256 devices in a mesh: row: 16 (over x, y), col: 8 (over z), depth: 2 (over core).
Axes of the slice: x: 4, y: 4, z: 8, core: 2. Of those that a mesh axis runs over, the one named last changes fastest.
Arguments:
- trailing: bfloat16 [24576, 24576], P('row', ('col', 'depth')), may hold values from -36 to 42, as said below
- earlier: bfloat16 [24576, 512], P('row', 'depth'), may hold values from -2 to 2
- block_order: int32 [48], replicated, may hold values from 0 to 47, each once
Outputs:
- panels: bfloat16 [24576, 1024], P('row', 'depth')
- schur_out: bfloat16 [24576, 24576], P('row', ('col', 'depth'))
The draws below stay inside these ranges and needn't reach their ends.
Inputs may be any that keep to these rules, and one draw needn't show every extreme that they name: `block_order`: each of the 48 tiles appears exactly once. Symmetric up to rounding; trailing - earlier earlier^T is positive definite.
All inputs are finite; a program needn't handle non-finite values.
Results may differ from the reference program's by a relative error of at most 0.0058.
Values may be sent and summed in bfloat16 or wider, within the bound.
No kernel may reach another device: no remote copies, remote signals or barrier semaphores. Data moves between devices by JAX's collectives and lax.ppermute only.
A program may use at most 128 MiB of HBM per device.

```python
import math
import jax
import jax.numpy as jnp
from jax import lax

M = 24576
B = 512
EARLIER = 512
NT = 48


def common_draws(key):
    first_key = jax.random.fold_in(key, 0)
    normal_part = jax.random.normal(first_key, (M, EARLIER), jnp.float32)
    return normal_part


def site_points(key):
    site_ids = jnp.arange(M, dtype=jnp.int32)
    east_cell = jnp.zeros((M,), jnp.int32)
    north_cell = jnp.zeros((M,), jnp.int32)
    for level_bit in range(8):
        east_bit = jnp.bitwise_and(jnp.right_shift(site_ids, 2 * level_bit), 1)
        north_bit = jnp.bitwise_and(jnp.right_shift(site_ids, 2 * level_bit + 1), 1)
        east_cell = east_cell + jnp.left_shift(east_bit, level_bit)
        north_cell = north_cell + jnp.left_shift(north_bit, level_bit)
    jitter = jax.random.uniform(key, (2, M), jnp.float32)
    spacing = 1.0 / math.sqrt(M)
    east = (east_cell.astype(jnp.float32) + jitter[0]) * spacing
    north = (north_cell.astype(jnp.float32) + jitter[1]) * spacing
    return jnp.stack([east, north], 0)


def draw_earlier(key, part):
    normal_part = common_draws(key)
    base_draw = jnp.clip(normal_part, -3.0, 3.0)
    return (base_draw * (2.0 / math.sqrt(EARLIER))).astype(jnp.bfloat16)


def draw_trailing(key, part):
    normal_part = common_draws(key)
    key = jax.random.fold_in(key, 5)
    site_key, nugget_key = jax.random.split(key)
    points = site_points(site_key)
    level = jax.random.uniform(nugget_key, (M,), jnp.float32)
    base_draw = jnp.clip(normal_part, -3.0, 3.0)
    nugget = 0.5 * jnp.exp(level * math.log(6.0))
    broad_sill = 0.5
    factors = (base_draw * (2.0 / math.sqrt(EARLIER))).astype(jnp.bfloat16).astype(jnp.float32)
    length_scale = 4.0 / math.sqrt(M)
    broad_scale = 0.5
    site_ids = jnp.arange(M, dtype=jnp.int32)

    def row_tile(tile_id):
        first_row = tile_id * B
        nearby = lax.dynamic_slice_in_dim(points, first_row, B, 1)
        gap_east = nearby[0][:, None] - points[0][None, :]
        gap_north = nearby[1][:, None] - points[1][None, :]
        distance = jnp.sqrt(gap_east * gap_east + gap_north * gap_north)
        scaled = math.sqrt(3.0) * distance / length_scale
        broad = math.sqrt(3.0) * distance / broad_scale
        values = (1.0 + scaled) * jnp.exp(-scaled) + broad_sill * (1.0 + broad) * jnp.exp(-broad)
        row_ids = first_row + jnp.arange(B, dtype=jnp.int32)
        own_nugget = lax.dynamic_slice_in_dim(nugget, first_row, B, 0)
        values = values + jnp.where(row_ids[:, None] == site_ids[None, :], own_nugget[:, None], 0.0)
        own_factors = lax.dynamic_slice_in_dim(factors, first_row, B, 0)
        values = values + jnp.dot(own_factors, factors.T, precision=lax.Precision.HIGHEST)
        return values.astype(jnp.bfloat16)
    return lax.map(row_tile, jnp.arange(M // B, dtype=jnp.int32)).reshape(M, M)


def setup_inputs(seed: int = 0) -> dict:
    arg_keys = jax.random.split(jax.random.key(seed), 4)
    return {
        "trailing": draw_trailing(jax.random.fold_in(arg_keys[3], 71), 0),
        "earlier": draw_earlier(jax.random.fold_in(arg_keys[3], 71), 0),
        "block_order": jax.random.permutation(arg_keys[2], NT).astype(jnp.int32),
    }


def make_panel(column, corner, pivot_tile, finished, tile_ids):
    factor = jnp.linalg.cholesky(corner)
    solved = jax.scipy.linalg.solve_triangular(factor, column.T, lower=True).T
    per_row = jnp.repeat(tile_ids, B, total_repeat_length=column.shape[0])
    stacked = jnp.tile(factor, (tile_ids.shape[0], 1))
    result = jnp.where((per_row == pivot_tile)[:, None], stacked, solved)
    for prior_tile in finished:
        result = jnp.where((per_row == prior_tile)[:, None], jnp.zeros_like(result), result)
    return result.astype(jnp.bfloat16)

def reference(trailing, earlier, block_order):
    tile_count = M // B
    tile_ids = jnp.arange(tile_count, dtype=jnp.int32)
    first_pivot = block_order[0].astype(jnp.int32)
    second_pivot = block_order[1].astype(jnp.int32)

    def current_column(pivot_tile):
        first_row = (pivot_tile * B).astype(jnp.int32)
        lead_cols = lax.dynamic_slice_in_dim(trailing, first_row, B, 1).astype(jnp.float32)
        factor_rows = lax.dynamic_slice_in_dim(earlier, first_row, B, 0)
        return lead_cols - jnp.dot(earlier.astype(jnp.float32), factor_rows.T.astype(jnp.float32), preferred_element_type=jnp.float32)
    column = current_column(first_pivot)
    corner = lax.dynamic_slice_in_dim(column, (first_pivot * B).astype(jnp.int32), B, 0)
    first_panel = make_panel(column, corner, first_pivot, [], tile_ids)
    pivot_rows = lax.dynamic_slice_in_dim(first_panel, (second_pivot * B).astype(jnp.int32), B, 0)
    column = current_column(second_pivot) - jnp.dot(first_panel.astype(jnp.float32), pivot_rows.T.astype(jnp.float32), preferred_element_type=jnp.float32)
    corner = lax.dynamic_slice_in_dim(column, (second_pivot * B).astype(jnp.int32), B, 0)
    second_panel = make_panel(column, corner, second_pivot, [first_pivot], tile_ids)
    col_tiles = jnp.repeat(tile_ids, B, total_repeat_length=M)
    col_kept = jnp.logical_and(col_tiles != first_pivot, col_tiles != second_pivot)

    def one_block(tile_id):
        first_row = (tile_id * B).astype(jnp.int32)
        row_block = lax.dynamic_slice_in_dim(trailing, first_row, B, 0).astype(jnp.float32)
        factor_rows = lax.dynamic_slice_in_dim(earlier, first_row, B, 0)
        row_block = row_block - jnp.dot(factor_rows.astype(jnp.float32), earlier.T.astype(jnp.float32), preferred_element_type=jnp.float32)
        first_rows = lax.dynamic_slice_in_dim(first_panel, first_row, B, 0)
        row_block = row_block - jnp.dot(first_rows.astype(jnp.float32), first_panel.T.astype(jnp.float32), preferred_element_type=jnp.float32)
        second_rows = lax.dynamic_slice_in_dim(second_panel, first_row, B, 0)
        row_block = row_block - jnp.dot(second_rows.astype(jnp.float32), second_panel.T.astype(jnp.float32), preferred_element_type=jnp.float32)
        row_kept = jnp.logical_and(tile_id != first_pivot, tile_id != second_pivot)
        kept_mask = jnp.logical_and(row_kept, col_kept)
        row_block = jnp.where(kept_mask[None, :], row_block, jnp.zeros_like(row_block))
        return row_block.astype(jnp.bfloat16)
    blocks = lax.map(one_block, tile_ids)
    schur_out = blocks.reshape(M, M)
    panels = jnp.concatenate([first_panel, second_panel], 1)
    return (panels, schur_out)
```

```python
import jax
import jax.numpy as jnp
from jax import lax
from jax.experimental import pallas as pl
from jax.experimental.pallas import tpu as pltpu
from jax.sharding import PartitionSpec as P

B = 512
F32 = jnp.float32
BF16 = jnp.bfloat16
HIGHEST = lax.Precision.HIGHEST


def pivot_block(d):
    n = 8
    d = [row[:] for row in d]
    low = [[None] * n for _ in range(n)]
    inv = [None] * n
    diag = [None] * n
    for j in range(0, n, 2):
        a, b, c = d[j][j], d[j + 1][j], d[j + 1][j + 1]
        det = a * c - b * b
        inv[j] = 1.0 / a
        inv_det = 1.0 / det
        inv[j + 1] = a * inv_det
        diag[j] = a
        diag[j + 1] = det * inv[j]
        low[j + 1][j] = b * inv[j]
        for i in range(j + 2, n):
            low[i][j] = d[i][j] * inv[j]
            low[i][j + 1] = (a * d[i][j + 1] - b * d[i][j]) * inv_det
        for i in range(j + 2, n):
            first = (c * d[i][j] - b * d[i][j + 1]) * inv_det
            for k in range(j + 2, i + 1):
                d[i][k] = d[i][k] - (first * d[k][j] + low[i][j + 1] * d[k][j + 1])
    return low, inv, diag


def chol_128(work, upper, base):
    lane = lax.broadcasted_iota(jnp.int32, (8, 128), 1)
    blocks = [work[base + 8 * m : base + 8 * m + 8, base : base + 128] for m in range(16)]

    def over_lanes(x, k):
        return jnp.broadcast_to(x[:, k : k + 1], (8, 128))

    def over_rows(x, k):
        return jnp.broadcast_to(x[k : k + 1, :], (8, 128))

    for q in range(16):
        o = 8 * q
        pivot = blocks[q]
        cols = [over_lanes(pivot, o + j) for j in range(8)]
        entries = [[over_rows(cols[j], i) if j <= i else None for j in range(8)] for i in range(8)]
        low, inv, diag = pivot_block(entries)
        inside = (lane >= o) & (lane < o + 8)
        solved = []
        for j in range(8):
            u = jnp.where(inside, jnp.where(lane == o + j, 1.0, 0.0), over_rows(pivot, j))
            for i in range(j):
                u = u - low[j][i] * solved[i]
            solved.append(u)
        if q < 15:
            back = [None] * 8
            for i in reversed(range(8)):
                g = solved[i] * inv[i]
                for j in range(i + 1, 8):
                    g = g - low[j][i] * back[j]
                back[i] = g
            for m in range(q + 1, 16):
                x = blocks[m]
                acc = jnp.where(inside, 0.0, x)
                for i in range(8):
                    acc = acc - over_lanes(x, o + i) * back[i]
                blocks[m] = acc
        for j in range(8):
            scale = lax.rsqrt(diag[j])
            root = diag[j] * scale
            row = solved[j] * scale
            up = jnp.where(lane < o + 8, 0.0, row)
            up = jnp.where(lane == o + j, root, up)
            for i in range(j + 1, 8):
                up = jnp.where(lane == o + i, low[i][j] * root, up)
            upper[base + o + j : base + o + j + 1, base : base + 128] = up[0:1]
            work[base + o + j : base + o + j + 1, base : base + 128] = jnp.where(lane <= o + j, row, 0.0)[0:1]


def dot(a, b, ca, cb, precision=None):
    return lax.dot_general(a, b, (((ca,), (cb,)), ((), ())), precision=precision, preferred_element_type=F32)


def chol_512(work, upper):
    upper[...] = jnp.zeros_like(upper)
    for b in range(4):
        o = 128 * b
        e = o + 128
        chol_128(work, upper, o)
        inv = work[o:e, o:e]
        if b > 0:
            work[o:e, 0:o] = dot(inv, work[o:e, 0:o], 1, 0, HIGHEST)
        if b < 3:
            up = dot(inv, work[o:e, e:B], 1, 0, HIGHEST)
            upper[o:e, e:B] = up
            work[o:e, e:B] = jnp.zeros_like(up)
            work[e:B, o:e] = jnp.zeros((B - e, 128), F32)
            work[e:B, 0:e] = work[e:B, 0:e] - dot(up, work[o:e, 0:e], 0, 0, HIGHEST)
            work[e:B, e:B] = work[e:B, e:B] - dot(up, up, 0, 0, HIGHEST)


def split(x):
    hi = x.astype(BF16)
    return hi, (x - hi.astype(F32)).astype(BF16)


def dot3(a, b, ca, cb):
    return dot(a[0], b[0], ca, cb) + (dot(a[0], b[1], ca, cb) + dot(a[1], b[0], ca, cb))


def symmetric(x):
    return 0.5 * (x + x.T)


def pivots_kernel(t00, t10, t11, ep0, ep1, f0, i0h, i0l, lp1, f1, i1h, i1l, work, upper):
    def finish(f, ih, il):
        f[...] = upper[...].T.astype(BF16)
        h, l = split(work[...])
        ih[...] = h
        il[...] = l

    work[...] = symmetric(t00[...].astype(F32) - dot(ep0[...], ep0[...], 1, 1))
    chol_512(work, upper)
    finish(f0, i0h, i0l)
    c10 = t10[...].astype(F32) - dot(ep1[...], ep0[...], 1, 1)
    lp1[...] = dot3(split(c10), (i0h[...], i0l[...]), 1, 1).astype(BF16)
    work[...] = symmetric(
        t11[...].astype(F32) - dot(ep1[...], ep1[...], 1, 1) - dot(lp1[...], lp1[...], 1, 1)
    )
    chol_512(work, upper)
    finish(f1, i1h, i1l)


def pivots(t00, t10, t11, ep0, ep1):
    tile = jax.ShapeDtypeStruct((B, B), BF16)
    return pl.pallas_call(
        pivots_kernel,
        out_shape=[tile] * 7,
        in_specs=[pl.BlockSpec(memory_space=pltpu.VMEM)] * 5,
        out_specs=[pl.BlockSpec(memory_space=pltpu.VMEM)] * 7,
        scratch_shapes=[pltpu.VMEM((B, B), F32)] * 2,
        compiler_params=pltpu.CompilerParams(vmem_limit_bytes=40 << 20),
        cost_estimate=pl.CostEstimate(flops=10**9, bytes_accessed=5 << 20, transcendentals=0),
        name="pivots",
    )(t00, t10, t11, ep0, ep1)


def update_kernel(
    info, trailing, a0, a1, er, r0, r1, eg, ep0, ep1, f0, i0h, i0l, lp1, f1, i1h, i1l,
    panels, out, l0t, l1t,
):
    step = pl.program_id(0)
    p0, p1 = info[0], info[1]
    i0 = (i0h[...], i0l[...])
    i1 = (i1h[...], i1l[...])

    @pl.when(step == 0)
    def _():
        for t in range(3):
            cols = slice(t * B, t * B + B)
            c0 = r0[:, cols].astype(F32) - dot(ep0[...], eg[cols, :], 1, 1)
            l0 = dot3(i0, split(c0), 1, 0).astype(BF16)
            l0t[:, cols] = l0
            c1 = r1[:, cols].astype(F32) - dot(ep1[...], eg[cols, :], 1, 1) - dot(lp1[...], l0, 1, 0)
            l1t[:, cols] = dot3(i1, split(c1), 1, 0).astype(BF16)

    tile = info[2] * 3 + step
    c0 = a0[...].astype(F32) - dot(er[...], ep0[...], 1, 1)
    l0 = dot3(split(c0), i0, 1, 1).astype(BF16)
    l0 = jnp.where(tile == p0, f0[...], l0)
    c1 = a1[...].astype(F32) - dot(er[...], ep1[...], 1, 1) - dot(l0, lp1[...], 1, 1)
    l1 = dot3(split(c1), i1, 1, 1).astype(BF16)
    l1 = jnp.where(tile == p1, f1[...], l1)
    l1 = jnp.where(tile == p0, jnp.zeros_like(l1), l1)
    panels[...] = jnp.where(info[4] == 0, l0, l1)
    row_kept = jnp.logical_and(tile != p0, tile != p1)
    for t in range(3):
        cols = slice(t * B, t * B + B)
        col_tile = info[3] * 3 + t
        kept = jnp.logical_and(row_kept, jnp.logical_and(col_tile != p0, col_tile != p1))
        c = trailing[:, cols].astype(F32) - (
            dot(er[...], eg[cols, :], 1, 1) + dot(l0, l0t[:, cols], 1, 0) + dot(l1, l1t[:, cols], 1, 0)
        )
        out[:, cols] = jnp.where(kept, c, 0.0).astype(BF16)


def update(info, trailing, a0, a1, er, r0, r1, eg, ep0, ep1, factors):
    n = trailing.shape[0]

    def rows(width):
        return pl.BlockSpec((B, width), lambda i, s: (i, 0))

    def whole(shape):
        return pl.BlockSpec(shape, lambda i, s: (0, 0))

    return pl.pallas_call(
        update_kernel,
        out_shape=[jax.ShapeDtypeStruct((n, B), BF16), jax.ShapeDtypeStruct((n, n), BF16)],
        grid_spec=pltpu.PrefetchScalarGridSpec(
            num_scalar_prefetch=1,
            grid=(3,),
            in_specs=[rows(n), rows(B), rows(B), rows(B), whole((B, n)), whole((B, n)), whole((n, B))]
            + [whole((B, B))] * 9,
            out_specs=[rows(B), rows(n)],
            scratch_shapes=[pltpu.VMEM((B, n), BF16)] * 2,
        ),
        compiler_params=pltpu.CompilerParams(vmem_limit_bytes=56 << 20),
        cost_estimate=pl.CostEstimate(flops=25 * 10**9, bytes_accessed=24 << 20, transcendentals=0),
        name="update",
    )(info, trailing, a0, a1, er, r0, r1, eg, ep0, ep1, *factors)


def gray(x, bit):
    return ((x >> bit) ^ (x >> (bit + 1))) & 1


def coord(index, mask):
    low = {1: 0, 3: 1, 4: 0, 12: 1}[mask]
    part = index & 3 if mask < 4 else index >> 2
    return gray(part, low)


ORDERS = ((1, 3, 4, 12), (3, 1, 12, 4), (4, 12, 1, 3), (12, 4, 3, 1))


def swap(x, axis, mask):
    size = lax.axis_size(axis)
    return lax.ppermute(x, axis, [(i, i ^ mask) for i in range(size)])


def plane_scatter(pieces, roots, me):
    pieces = list(pieces)
    for t in range(4):
        sent, kept = [], []
        for x, order in zip(pieces, ORDERS):
            c = coord(me, order[t])
            half = x.shape[0] // 2
            sent.append(lax.dynamic_slice_in_dim(x, (1 - c) * half, half, 0))
            kept.append(lax.dynamic_slice_in_dim(x, c * half, half, 0))
        got = [swap(x, "row", order[t]) for x, order in zip(sent, ORDERS)]
        pieces = [
            jnp.where(coord(root, order[t]) != coord(me, order[t]), g, k)
            for g, k, root, order in zip(got, kept, roots, ORDERS)
        ]
    return pieces


def plane_gather(pieces, me):
    for t in reversed(range(4)):
        got = [swap(x, "row", order[t]) for x, order in zip(pieces, ORDERS)]
        pieces = [
            jnp.where(coord(me, order[t]) == 0, jnp.concatenate([x, g], 0), jnp.concatenate([g, x], 0))
            for g, x, order in zip(got, pieces, ORDERS)
        ]
    return pieces


def col_spread(pieces, roots, me):
    for bit, mask in ((0, 1), (1, 3), (2, 7)):
        got = [swap(x, "col", mask) for x in pieces]
        pieces = [
            jnp.where(gray(root, bit) != gray(me, bit), g, x) for g, x, root in zip(got, pieces, roots)
        ]
    return pieces


def lane_values(values, width):
    return jnp.repeat(jnp.stack(values).astype(jnp.int32), width, total_repeat_length=len(values) * width)[None, :]


def cut(x, widths):
    at, out = 0, []
    for w in widths:
        out.append(x[:, at : at + w])
        at += w
    return out


def body(trailing, earlier, block_order):
    z = lax.axis_index("col")
    d = lax.axis_index("depth")
    r = lax.axis_index("row")
    g = 2 * z + d
    n = trailing.shape[0]
    count = n // B
    p0, p1 = block_order[0], block_order[1]
    q0, q1 = p0 // count, p1 // count
    s0, s1 = p0 % count * B, p1 % count * B
    half = B // 2

    def tile(rows, cols):
        return lax.dynamic_slice(trailing, (rows, cols), (B, B))

    cands = [tile(s0, s0), tile(s1, s0), tile(s1, s1)]
    owners = [q0, q0, q1]

    def half_of(x, which):
        return lax.dynamic_slice_in_dim(x, which * half, half, 1)

    got = swap(jnp.concatenate([half_of(x, 1 - d) for x in cands], 1), "depth", 1)
    mine = jnp.concatenate([half_of(x, d) for x in cands], 1)
    owner_core = lane_values([q & 1 for q in owners], half)
    tiles = jnp.where(owner_core == d, mine, got)
    ep = [lax.dynamic_slice_in_dim(earlier, s, B, 0) for s in (s0, s1)]
    payload = jnp.concatenate([tiles] + ep, 1)
    widths = (384, 384, 256, 256)
    row_roots = cut(lane_values([q0, q1, q1, q0, q1], half), widths)
    col_roots = cut(lane_values([q0 >> 1, q0 >> 1, q1 >> 1, z, z], half), widths)
    pieces = plane_scatter(cut(payload, widths), row_roots, r)
    pieces = col_spread(pieces, col_roots, z)
    pieces = plane_gather(pieces, r)
    payload = jnp.concatenate(pieces, 1)
    other = swap(payload, "depth", 1)
    first = jnp.where(d == 0, payload, other)
    second = jnp.where(d == 0, other, payload)
    t00, t10, t11, ep0, ep1 = [
        jnp.concatenate([first[:, i * half : (i + 1) * half], second[:, i * half : (i + 1) * half]], 1)
        for i in range(5)
    ]

    cands = [lax.dynamic_slice_in_dim(trailing, s, B, 1) for s in (s0, s1)]
    got = swap(jnp.concatenate([half_of(x, 1 - d) for x in cands], 1), "depth", 1)
    mine = jnp.concatenate([half_of(x, d) for x in cands], 1)
    column = jnp.where(lane_values([q0 & 1, q1 & 1], half) == d, mine, got)
    column = jnp.where(lane_values([q0 >> 1, q1 >> 1], half) == z, column, jnp.zeros_like(column))
    column = lax.psum(column, "col")
    other = swap(column, "depth", 1)
    first = jnp.where(d == 0, column, other)
    second = jnp.where(d == 0, other, column)
    a0, a1 = [
        jnp.concatenate([first[:, i * half : (i + 1) * half], second[:, i * half : (i + 1) * half]], 1)
        for i in range(2)
    ]

    rows0 = lax.dynamic_slice_in_dim(trailing, s0, B, 0)
    rows1 = lax.dynamic_slice_in_dim(trailing, s1, B, 0)
    flat = jnp.concatenate([earlier[i * B : (i + 1) * B] for i in range(count)], 1)
    payload = jnp.concatenate([rows0, rows1, flat, flat], 1)
    w = payload.shape[1] // 4
    roots = jnp.concatenate(
        [lane_values([q0, q1], n), lane_values([2 * z, 2 * z + 1], flat.shape[1])], 1
    )
    pieces = plane_scatter(cut(payload, (w,) * 4), cut(roots, (w,) * 4), r)
    pieces = plane_gather(pieces, r)
    payload = jnp.concatenate(pieces, 1)
    rows0 = payload[:, :n]
    rows1 = payload[:, n : 2 * n]
    fw = flat.shape[1]
    e_even = payload[:, 2 * n : 2 * n + fw]
    e_odd = payload[:, 2 * n + fw :]
    keep = jnp.where(d == 0, e_even, e_odd)
    got = swap(jnp.where(d == 0, e_odd, e_even), "depth", 1)

    def unflat(x):
        return jnp.concatenate([x[:, i * half : (i + 1) * half] for i in range(count)], 0)

    keep, got = unflat(keep), unflat(got)
    eg = jnp.where(d == 0, jnp.concatenate([keep, got], 1), jnp.concatenate([got, keep], 1))
    got = swap(earlier, "depth", 1)
    er = jnp.where(d == 0, jnp.concatenate([earlier, got], 1), jnp.concatenate([got, earlier], 1))

    factors = pivots(t00, t10, t11, ep0, ep1)
    info = jnp.stack([p0, p1, r, g, d]).astype(jnp.int32)
    panels, out = update(info, trailing, a0, a1, er, rows0, rows1, eg, ep0, ep1, factors)
    return panels, out


def solution(mesh):
    placed = (P("row", ("col", "depth")), P("row", "depth"), P())
    return jax.shard_map(
        body,
        mesh=mesh,
        in_specs=placed,
        out_specs=(P("row", "depth"), P("row", ("col", "depth"))),
        check_vma=False,
    )
```

```python
import jax
import jax.numpy as jnp
from jax import lax
from jax.experimental import pallas as pl
from jax.experimental.pallas import tpu as pltpu
from jax.sharding import PartitionSpec as P

B = 512
F32 = jnp.float32
BF16 = jnp.bfloat16
HIGHEST = lax.Precision.HIGHEST


def pivot_block(d):
    n = 8
    d = [row[:] for row in d]
    low = [[None] * n for _ in range(n)]
    inv = [None] * n
    diag = [None] * n
    for j in range(0, n, 2):
        a, b, c = d[j][j], d[j + 1][j], d[j + 1][j + 1]
        det = a * c - b * b
        inv[j] = 1.0 / a
        inv_det = 1.0 / det
        inv[j + 1] = a * inv_det
        diag[j] = a
        diag[j + 1] = det * inv[j]
        low[j + 1][j] = b * inv[j]
        for i in range(j + 2, n):
            low[i][j] = d[i][j] * inv[j]
            low[i][j + 1] = (a * d[i][j + 1] - b * d[i][j]) * inv_det
        for i in range(j + 2, n):
            first = (c * d[i][j] - b * d[i][j + 1]) * inv_det
            for k in range(j + 2, i + 1):
                d[i][k] = d[i][k] - (first * d[k][j] + low[i][j + 1] * d[k][j + 1])
    return low, inv, diag


def chol_128(work, upper, base):
    lane = lax.broadcasted_iota(jnp.int32, (8, 128), 1)
    blocks = [work[base + 8 * m : base + 8 * m + 8, base : base + 128] for m in range(16)]

    def over_lanes(x, k):
        return jnp.broadcast_to(x[:, k : k + 1], (8, 128))

    def over_rows(x, k):
        return jnp.broadcast_to(x[k : k + 1, :], (8, 128))

    for q in range(16):
        o = 8 * q
        pivot = blocks[q]
        cols = [over_lanes(pivot, o + j) for j in range(8)]
        entries = [[over_rows(cols[j], i) if j <= i else None for j in range(8)] for i in range(8)]
        low, inv, diag = pivot_block(entries)
        inside = (lane >= o) & (lane < o + 8)
        solved = []
        for j in range(8):
            u = jnp.where(inside, jnp.where(lane == o + j, 1.0, 0.0), over_rows(pivot, j))
            for i in range(j):
                u = u - low[j][i] * solved[i]
            solved.append(u)
        if q < 15:
            back = [None] * 8
            for i in reversed(range(8)):
                g = solved[i] * inv[i]
                for j in range(i + 1, 8):
                    g = g - low[j][i] * back[j]
                back[i] = g
            for m in range(q + 1, 16):
                x = blocks[m]
                acc = jnp.where(inside, 0.0, x)
                for i in range(8):
                    acc = acc - over_lanes(x, o + i) * back[i]
                blocks[m] = acc
        for j in range(8):
            scale = lax.rsqrt(diag[j])
            root = diag[j] * scale
            row = solved[j] * scale
            up = jnp.where(lane < o + 8, 0.0, row)
            up = jnp.where(lane == o + j, root, up)
            for i in range(j + 1, 8):
                up = jnp.where(lane == o + i, low[i][j] * root, up)
            upper[base + o + j : base + o + j + 1, base : base + 128] = up[0:1]
            work[base + o + j : base + o + j + 1, base : base + 128] = jnp.where(lane <= o + j, row, 0.0)[0:1]


def dot(a, b, ca, cb, precision=None):
    return lax.dot_general(a, b, (((ca,), (cb,)), ((), ())), precision=precision, preferred_element_type=F32)


def chol_strips(work, upper, strips):
    for b in strips:
        o = 128 * b
        e = o + 128
        chol_128(work, upper, o)
        inv = work[o:e, o:e]
        if b > 0:
            work[o:e, 0:o] = dot(inv, work[o:e, 0:o], 1, 0, HIGHEST)
            upper[o:e, 0:o] = jnp.zeros((128, o), F32)
        if b < 3:
            up = dot(inv, work[o:e, e:B], 1, 0, HIGHEST)
            upper[o:e, e:B] = up
            work[o:e, e:B] = jnp.zeros_like(up)
            work[e:B, o:e] = jnp.zeros((B - e, 128), F32)
            work[e:B, 0:e] = work[e:B, 0:e] - dot(up, work[o:e, 0:e], 0, 0, HIGHEST)
            work[e:B, e:B] = work[e:B, e:B] - dot(up, up, 0, 0, HIGHEST)


def split(x):
    hi = x.astype(BF16)
    return hi, (x - hi.astype(F32)).astype(BF16)


def dot3(a, b, ca, cb):
    return dot(a[0], b[0], ca, cb) + (dot(a[0], b[1], ca, cb) + dot(a[1], b[0], ca, cb))


def symmetric(x):
    return 0.5 * (x + x.T)


def by_core(info, own, other):
    first = info[4] == 0
    own, other = own.astype(F32), other.astype(F32)
    return jnp.concatenate([jnp.where(first, own, other), jnp.where(first, other, own)], 1)


HALF = B // 2


def payload_part(own, other, index):
    lanes = slice(index * HALF, index * HALF + HALF)
    return own[:, lanes], other[:, lanes]


def payload_tile(info, own, other, index):
    return by_core(info, *payload_part(own, other, index))


def payload_rows(own, other, index):
    return jnp.concatenate(payload_part(own, other, index), 1)


def finish(work, upper, f, ih, il):
    f[...] = upper[...].T.astype(BF16)
    h, l = split(work[...])
    ih[...] = h
    il[...] = l


def first_open(info, own, other, work, upper):
    ep0 = payload_rows(own, other, 1)
    work[...] = symmetric(payload_tile(info, own, other, 0) - dot(ep0, ep0, 1, 1))
    upper[...] = jnp.zeros_like(upper)
    chol_strips(work, upper, (0, 1))


def first_close(info, own, other, work_in, upper_in, f, ih, il, lp, next_work, work, upper):
    work[...] = work_in[...]
    upper[...] = upper_in[...]
    chol_strips(work, upper, (2, 3))
    finish(work, upper, f, ih, il)
    ep0 = payload_rows(own, other, 1)
    ep1 = payload_rows(own, other, 3)
    c10 = payload_tile(info, own, other, 2) - dot(ep1, ep0, 1, 1)
    lp[...] = dot3(split(c10), (ih[...], il[...]), 1, 1).astype(BF16)
    c11 = payload_tile(info, own, other, 4) - dot(ep1, ep1, 1, 1) - dot(lp[...], lp[...], 1, 1)
    next_work[...] = symmetric(c11)


def second_open(work_in, work, upper):
    work[...] = work_in[...]
    upper[...] = jnp.zeros_like(upper)
    chol_strips(work, upper, (0,))


def second_middle(work_in, upper_in, work, upper):
    work[...] = work_in[...]
    upper[...] = upper_in[...]
    chol_strips(work, upper, (1,))


def second_close(work_in, upper_in, f, ih, il, work, upper):
    work[...] = work_in[...]
    upper[...] = upper_in[...]
    chol_strips(work, upper, (2, 3))
    finish(work, upper, f, ih, il)


WIDE = jax.ShapeDtypeStruct((B, B), F32)
NARROW = jax.ShapeDtypeStruct((B, B), BF16)


def tile_call(kernel, out_shape, scratch, args, info=None):
    def spec(_):
        return pl.BlockSpec(memory_space=pltpu.VMEM)

    specs = [spec(a) for a in args]
    if info is not None:
        specs = [pl.BlockSpec(memory_space=pltpu.SMEM)] + specs
        args = [info] + list(args)
    return pl.pallas_call(
        kernel,
        out_shape=out_shape,
        in_specs=specs,
        out_specs=[spec(a) for a in out_shape],
        scratch_shapes=[pltpu.VMEM((B, B), F32)] * scratch,
        compiler_params=pltpu.CompilerParams(vmem_limit_bytes=32 << 20),
        cost_estimate=pl.CostEstimate(flops=10**10, bytes_accessed=4 << 20, transcendentals=0),
        name=kernel.__name__,
    )(*args)


def lanes_of(pieces, start, width):
    w = pieces[0].shape[1]
    out = []
    while width > 0:
        at = start % w
        take = min(width, w - at)
        out.append(pieces[start // w][:, at : at + take])
        start, width = start + take, width - take
    return out[0] if len(out) == 1 else jnp.concatenate(out, 1)


def update_kernel(
    info, trailing, col_own, col_oth, er_own, er_oth, q0, q1, q2, q3, eg_own, eg_oth, pay_own, pay_oth,
    f0, i0h, i0l, lp1, f1, i1h, i1l, panels, out, l0t, l1t,
):
    step = pl.program_id(0)
    p0, p1 = info[0], info[1]
    i0 = (i0h[...], i0l[...])
    i1 = (i1h[...], i1l[...])
    ep0 = payload_rows(pay_own, pay_oth, 1)
    ep1 = payload_rows(pay_own, pay_oth, 3)

    def eg(t):
        lanes = slice(t * HALF, t * HALF + HALF)
        return jnp.concatenate([eg_own[:, lanes], eg_oth[:, lanes]], 1)

    @pl.when(step == 0)
    def _():
        for t in range(3):
            cols = slice(t * B, t * B + B)
            c0 = lanes_of((q0, q1, q2, q3), t * B, B).astype(F32) - dot(ep0, eg(t), 1, 1)
            l0 = dot3(i0, split(c0), 1, 0).astype(BF16)
            l0t[:, cols] = l0
            c1 = lanes_of((q0, q1, q2, q3), 3 * B + t * B, B).astype(F32) - dot(ep1, eg(t), 1, 1)
            c1 = c1 - dot(lp1[...], l0, 1, 0)
            l1t[:, cols] = dot3(i1, split(c1), 1, 0).astype(BF16)

    tile = info[2] * 3 + step
    er = jnp.concatenate([er_own[...], er_oth[...]], 1)
    c0 = by_core(info, col_own[:, :HALF], col_oth[:, :HALF]) - dot(er, ep0, 1, 1)
    l0 = dot3(split(c0), i0, 1, 1).astype(BF16)
    l0 = jnp.where(tile == p0, f0[...], l0)
    c1 = by_core(info, col_own[:, HALF:], col_oth[:, HALF:]) - dot(er, ep1, 1, 1) - dot(l0, lp1[...], 1, 1)
    l1 = dot3(split(c1), i1, 1, 1).astype(BF16)
    l1 = jnp.where(tile == p1, f1[...], l1)
    l1 = jnp.where(tile == p0, jnp.zeros_like(l1), l1)
    panels[...] = jnp.where(info[4] == 0, l0, l1)
    row_kept = jnp.logical_and(tile != p0, tile != p1)
    for t in range(3):
        cols = slice(t * B, t * B + B)
        col_tile = info[3] * 3 + t
        kept = jnp.logical_and(row_kept, jnp.logical_and(col_tile != p0, col_tile != p1))
        c = trailing[:, cols].astype(F32) - (
            dot(er, eg(t), 1, 1) + dot(l0, l0t[:, cols], 1, 0) + dot(l1, l1t[:, cols], 1, 0)
        )
        out[:, cols] = jnp.where(kept, c, 0.0).astype(BF16)


def update(info, by_rows, whole):
    n = by_rows[0].shape[0]

    def rows(x):
        return pl.BlockSpec((B, x.shape[1]), lambda i, s: (i, 0))

    def all_of(x):
        return pl.BlockSpec(x.shape, lambda i, s: (0, 0))

    out_shape = [jax.ShapeDtypeStruct((n, B), BF16), jax.ShapeDtypeStruct((n, n), BF16)]
    return pl.pallas_call(
        update_kernel,
        out_shape=out_shape,
        grid_spec=pltpu.PrefetchScalarGridSpec(
            num_scalar_prefetch=1,
            grid=(n // B,),
            in_specs=[rows(x) for x in by_rows] + [all_of(x) for x in whole],
            out_specs=[rows(x) for x in out_shape],
            scratch_shapes=[pltpu.VMEM((B, n), BF16)] * 2,
        ),
        compiler_params=pltpu.CompilerParams(vmem_limit_bytes=56 << 20),
        cost_estimate=pl.CostEstimate(flops=25 * 10**9, bytes_accessed=24 << 20, transcendentals=0),
        name="update",
    )(info, *by_rows, *whole)


barrier = lax.optimization_barrier
ORDERS = ((1, 3, 4, 12), (3, 1, 12, 4), (4, 12, 1, 3), (12, 4, 3, 1))


def gray(x, bit):
    return ((x >> bit) ^ (x >> (bit + 1))) & 1


def coord(index, mask):
    part = index & 3 if mask < 4 else index >> 2
    return gray(part, {1: 0, 3: 1, 4: 0, 12: 1}[mask])


def swap(x, axis, mask):
    size = lax.axis_size(axis)
    return lax.ppermute(x, axis, [(i, i ^ mask) for i in range(size)])


def lane_roots(width, parts):
    lane = lax.broadcasted_iota(jnp.int32, (1, width), 1)
    out = jnp.full((1, width), parts[-1][1], jnp.int32)
    for end, root in reversed(parts[:-1]):
        out = jnp.where(lane < end, root, out)
    return out


def ring_take(chunks, step, me, root):
    sent = barrier(tuple(lax.dynamic_index_in_dim(chunks, me ^ k, 0, keepdims=False) for k in (1, 2, 3)))
    got = barrier(tuple(swap(x, "row", k * step) for x, k in zip(sent, (1, 2, 3))))
    out = lax.dynamic_index_in_dim(chunks, me, 0, keepdims=False)
    for k in (1, 2, 3):
        out = jnp.where((me ^ root) == k, got[k - 1], out)
    return out


def ring_join(x, step, me):
    got = barrier(tuple(swap(x, "row", k * step) for k in (1, 2, 3)))
    parts = []
    for k in range(4):
        other = me ^ k
        parts.append(
            jnp.where(other == 0, x, jnp.where(other == 1, got[0], jnp.where(other == 2, got[1], got[2])))
        )
    return jnp.concatenate(parts, 0)


def col_spread(x, me, root):
    got = barrier(tuple(swap(x, "col", k) for k in (1, 2, 3)))
    out = x
    for k in (1, 2, 3):
        out = jnp.where(((me ^ root) & 3) == k, got[k - 1], out)
    got = swap(out, "col", 7)
    return jnp.where((me >> 2) != (root >> 2), got, out)


class Plane:
    def __init__(self, pieces, roots, me):
        self.pieces, self.roots, self.me, self.step = list(pieces), roots, me, 0

    def masks(self):
        t = (0, 1, 2, 3, 1, 0)[self.step]
        return [order[t] for order in ORDERS]

    def outgoing(self):
        self.sent, self.kept = [], []
        for x, mask in zip(self.pieces, self.masks()):
            if self.step < 2:
                c = coord(self.me, mask)
                half = x.shape[0] // 2
                self.sent.append(lax.dynamic_slice_in_dim(x, (1 - c) * half, half, 0))
                self.kept.append(lax.dynamic_slice_in_dim(x, c * half, half, 0))
            else:
                self.sent.append(x)
                self.kept.append(x)
        return tuple(self.sent)

    def move(self, sent):
        if self.step >= 2:
            self.kept = sent
        return tuple(swap(x, "row", mask) for x, mask in zip(sent, self.masks()))

    def take(self, got):
        out = []
        for g, k, root, mask in zip(got, self.kept, self.roots, self.masks()):
            c = coord(self.me, mask)
            if self.step < 4:
                out.append(jnp.where(coord(root, mask) != c, g, k))
            else:
                out.append(jnp.where(c == 0, jnp.concatenate([k, g], 0), jnp.concatenate([g, k], 0)))
        self.pieces = out
        self.step += 1


def body(trailing, earlier, block_order):
    z = lax.axis_index("col")
    d = lax.axis_index("depth")
    r = lax.axis_index("row")
    g = 2 * z + d
    n = trailing.shape[0]
    count = n // B
    p0, p1 = block_order[0], block_order[1]
    g0, g1 = p0 // count, p1 // count
    s0, s1 = p0 % count * B, p1 % count * B
    info = jnp.stack([p0, p1, r, g, d]).astype(jnp.int32)

    def half_of(x, which):
        return lax.dynamic_slice_in_dim(x, which * HALF, HALF, 1)

    def core_halves(cands, cores):
        got = swap(jnp.concatenate([half_of(x, 1 - d) for x in cands], 1), "depth", 1)
        return [
            jnp.where(core == d, half_of(x, d), got[:, i * HALF : i * HALF + HALF])
            for i, (x, core) in enumerate(zip(cands, cores))
        ]

    def tile(rows, cols):
        return lax.dynamic_slice(trailing, (rows, cols), (B, B))

    t00, t10, t11 = core_halves([tile(s0, s0), tile(s1, s0), tile(s1, s1)], [g0 & 1, g0 & 1, g1 & 1])
    ep0 = lax.dynamic_slice_in_dim(earlier, s0, B, 0)
    ep1 = lax.dynamic_slice_in_dim(earlier, s1, B, 0)
    pay = jnp.concatenate([t00, ep0, t10, ep1, t11], 1)
    width = pay.shape[1]
    pay, s0, s1 = barrier((pay, s0, s1))
    row_root = lane_roots(width, [(2 * HALF, g0), (width, g1)])
    z0, z1 = g0 >> 1, g1 >> 1
    col_root = lane_roots(width, [(HALF, z0), (2 * HALF, z), (3 * HALF, z0), (4 * HALF, z), (width, z1)])
    x_here, y_here = r >> 2, r & 3

    cands = [lax.dynamic_slice_in_dim(trailing, s, B, 1) for s in (s0, s1)]
    a0, a1 = core_halves(cands, [g0 & 1, g1 & 1])
    column = jnp.concatenate(
        [jnp.where(z0 == z, a0, jnp.zeros_like(a0)), jnp.where(z1 == z, a1, jnp.zeros_like(a1))], 1
    )
    column, s0, s1 = barrier((column, s0, s1))
    column = lax.psum(column, "col")

    pay = ring_take(pay.reshape(4, B // 4, width), 1, y_here, row_root & 3)
    pay = ring_take(pay.reshape(4, B // 16, width), 4, x_here, row_root >> 2)

    rows0 = lax.dynamic_slice_in_dim(trailing, s0, B, 0)
    rows1 = lax.dynamic_slice_in_dim(trailing, s1, B, 0)
    flat = jnp.concatenate([earlier[i * B : (i + 1) * B] for i in range(count)], 1)
    fw = flat.shape[1]
    w = (n + fw) // 2
    pieces = [lanes_of_concat((rows0, rows1, flat, flat), i * w, w) for i in range(4)]
    ends = [(n, g0), (2 * n, g1), (2 * n + fw, 2 * z), (2 * n + 2 * fw, 2 * z + 1)]
    roots = [lane_roots(w, [(end - i * w, root) for end, root in ends]) for i in range(4)]
    plane = Plane(pieces, roots, r)
    pay, sent = barrier((pay, plane.outgoing()))
    got = plane.move(sent)
    pay = col_spread(pay, z, col_root)
    pay = ring_join(pay, 4, x_here)
    pay = ring_join(pay, 1, y_here)
    other = swap(pay, "depth", 1)
    er_other = swap(earlier, "depth", 1)
    pay, other, got = barrier((pay, other, got))

    def beside(state, kernel):
        nonlocal got
        plane.take(got)
        state, sent = barrier((state, plane.outgoing()))
        got = plane.move(sent)
        state, got = barrier((kernel(state), got))
        return state

    two = [WIDE, WIDE]
    state = beside((pay, other), lambda s: tuple(tile_call(first_open, two, 0, s, info)))
    f0, i0h, i0l, lp1, work = beside(
        state,
        lambda s: tuple(tile_call(first_close, [NARROW] * 4 + [WIDE], 2, (pay, other) + tuple(s), info)),
    )
    state = beside((work,), lambda s: tuple(tile_call(second_open, two, 0, s)))
    state = beside(state, lambda s: tuple(tile_call(second_middle, two, 0, s)))
    state, column = barrier((state, column))
    column_other = swap(column, "depth", 1)
    f1, i1h, i1l = beside(state, lambda s: tuple(tile_call(second_close, [NARROW] * 3, 2, s)))
    plane.take(got)
    last = plane.pieces
    even = lanes_of_concat(last, 2 * n, fw)
    odd = lanes_of_concat(last, 2 * n + fw, fw)
    eg = jnp.where(d == 0, even, odd)
    eg_other = swap(jnp.where(d == 0, odd, even), "depth", 1)
    panels, out = update(
        info,
        [trailing, column, column_other, earlier, er_other],
        list(last) + [eg, eg_other, pay, other, f0, i0h, i0l, lp1, f1, i1h, i1l],
    )
    return panels, out


def lanes_of_concat(arrays, start, width):
    out, at = [], 0
    for x in arrays:
        lo, hi = max(start, at), min(start + width, at + x.shape[1])
        if lo < hi:
            out.append(x[:, lo - at : hi - at])
        at += x.shape[1]
    return out[0] if len(out) == 1 else jnp.concatenate(out, 1)


def solution(mesh):
    placed = (P("row", ("col", "depth")), P("row", "depth"), P())
    return jax.shard_map(
        body,
        mesh=mesh,
        in_specs=placed,
        out_specs=(P("row", "depth"), P("row", ("col", "depth"))),
        check_vma=False,
    )
```

```python
import jax
import jax.numpy as jnp
from jax import lax
from jax.experimental import pallas as pl
from jax.experimental.pallas import tpu as pltpu
from jax.sharding import PartitionSpec as P

B = 512
F32 = jnp.float32
BF16 = jnp.bfloat16
HIGHEST = lax.Precision.HIGHEST


def pivot_block(d):
    n = 8
    d = [row[:] for row in d]
    low = [[None] * n for _ in range(n)]
    inv = [None] * n
    diag = [None] * n
    for j in range(0, n, 2):
        a, b, c = d[j][j], d[j + 1][j], d[j + 1][j + 1]
        det = a * c - b * b
        inv[j] = 1.0 / a
        inv_det = 1.0 / det
        inv[j + 1] = a * inv_det
        diag[j] = a
        diag[j + 1] = det * inv[j]
        low[j + 1][j] = b * inv[j]
        for i in range(j + 2, n):
            low[i][j] = d[i][j] * inv[j]
            low[i][j + 1] = (a * d[i][j + 1] - b * d[i][j]) * inv_det
        for i in range(j + 2, n):
            first = (c * d[i][j] - b * d[i][j + 1]) * inv_det
            for k in range(j + 2, i + 1):
                d[i][k] = d[i][k] - (first * d[k][j] + low[i][j + 1] * d[k][j + 1])
    return low, inv, diag


def chol_128(work, upper, base):
    lane = lax.broadcasted_iota(jnp.int32, (8, 128), 1)
    blocks = [work[base + 8 * m : base + 8 * m + 8, base : base + 128] for m in range(16)]

    def over_lanes(x, k):
        return jnp.broadcast_to(x[:, k : k + 1], (8, 128))

    def over_rows(x, k):
        return jnp.broadcast_to(x[k : k + 1, :], (8, 128))

    for q in range(16):
        o = 8 * q
        pivot = blocks[q]
        cols = [over_lanes(pivot, o + j) for j in range(8)]
        entries = [[over_rows(cols[j], i) if j <= i else None for j in range(8)] for i in range(8)]
        low, inv, diag = pivot_block(entries)
        inside = (lane >= o) & (lane < o + 8)
        solved = []
        for j in range(8):
            u = jnp.where(inside, jnp.where(lane == o + j, 1.0, 0.0), over_rows(pivot, j))
            for i in range(j):
                u = u - low[j][i] * solved[i]
            solved.append(u)
        if q < 15:
            back = [None] * 8
            for i in reversed(range(8)):
                g = solved[i] * inv[i]
                for j in range(i + 1, 8):
                    g = g - low[j][i] * back[j]
                back[i] = g
            for m in range(q + 1, 16):
                x = blocks[m]
                acc = jnp.where(inside, 0.0, x)
                for i in range(8):
                    acc = acc - over_lanes(x, o + i) * back[i]
                blocks[m] = acc
        for j in range(8):
            scale = lax.rsqrt(diag[j])
            root = diag[j] * scale
            row = solved[j] * scale
            up = jnp.where(lane < o + 8, 0.0, row)
            up = jnp.where(lane == o + j, root, up)
            for i in range(j + 1, 8):
                up = jnp.where(lane == o + i, low[i][j] * root, up)
            upper[base + o + j : base + o + j + 1, base : base + 128] = up[0:1]
            work[base + o + j : base + o + j + 1, base : base + 128] = jnp.where(lane <= o + j, row, 0.0)[0:1]


def dot(a, b, ca, cb, precision=None):
    return lax.dot_general(a, b, (((ca,), (cb,)), ((), ())), precision=precision, preferred_element_type=F32)


def chol_strips(work, upper, strips):
    for b in strips:
        o = 128 * b
        e = o + 128
        chol_128(work, upper, o)
        inv = work[o:e, o:e]
        if b > 0:
            work[o:e, 0:o] = dot(inv, work[o:e, 0:o], 1, 0, HIGHEST)
            upper[o:e, 0:o] = jnp.zeros((128, o), F32)
        if b < 3:
            up = dot(inv, work[o:e, e:B], 1, 0, HIGHEST)
            upper[o:e, e:B] = up
            work[o:e, e:B] = jnp.zeros_like(up)
            work[e:B, o:e] = jnp.zeros((B - e, 128), F32)
            work[e:B, 0:e] = work[e:B, 0:e] - dot(up, work[o:e, 0:e], 0, 0, HIGHEST)
            work[e:B, e:B] = work[e:B, e:B] - dot(up, up, 0, 0, HIGHEST)


def split(x):
    hi = x.astype(BF16)
    return hi, (x - hi.astype(F32)).astype(BF16)


def dot3(a, b, ca, cb):
    return dot(a[0], b[0], ca, cb) + (dot(a[0], b[1], ca, cb) + dot(a[1], b[0], ca, cb))


def symmetric(x):
    return 0.5 * (x + x.T)


def by_core(info, own, other):
    first = info[4] == 0
    own, other = own.astype(F32), other.astype(F32)
    return jnp.concatenate([jnp.where(first, own, other), jnp.where(first, other, own)], 1)


HALF = B // 2


def payload_part(own, other, index):
    lanes = slice(index * HALF, index * HALF + HALF)
    return own[:, lanes], other[:, lanes]


def payload_tile(info, own, other, index):
    return by_core(info, *payload_part(own, other, index))


def payload_rows(own, other, index):
    return jnp.concatenate(payload_part(own, other, index), 1)


def finish(work, upper, f, ih, il):
    f[...] = upper[...].T.astype(BF16)
    h, l = split(work[...])
    ih[...] = h
    il[...] = l


def first_factor(info, own, other, f, ih, il, lp, next_work, work, upper):
    ep0 = payload_rows(own, other, 1)
    ep1 = payload_rows(own, other, 3)
    work[...] = symmetric(payload_tile(info, own, other, 0) - dot(ep0, ep0, 1, 1))
    chol_strips(work, upper, (0, 1, 2, 3))
    finish(work, upper, f, ih, il)
    c10 = payload_tile(info, own, other, 2) - dot(ep1, ep0, 1, 1)
    lp[...] = dot3(split(c10), (ih[...], il[...]), 1, 1).astype(BF16)
    c11 = payload_tile(info, own, other, 4) - dot(ep1, ep1, 1, 1) - dot(lp[...], lp[...], 1, 1)
    next_work[...] = symmetric(c11)


def second_factor(work_in, f, ih, il, work, upper):
    work[...] = work_in[...]
    chol_strips(work, upper, (0, 1, 2, 3))
    finish(work, upper, f, ih, il)


WIDE = jax.ShapeDtypeStruct((B, B), F32)
NARROW = jax.ShapeDtypeStruct((B, B), BF16)


def tile_call(kernel, out_shape, scratch, args, info=None):
    def spec(_):
        return pl.BlockSpec(memory_space=pltpu.VMEM)

    specs = [spec(a) for a in args]
    if info is not None:
        specs = [pl.BlockSpec(memory_space=pltpu.SMEM)] + specs
        args = [info] + list(args)
    return pl.pallas_call(
        kernel,
        out_shape=out_shape,
        in_specs=specs,
        out_specs=[spec(a) for a in out_shape],
        scratch_shapes=[pltpu.VMEM((B, B), F32)] * scratch,
        compiler_params=pltpu.CompilerParams(vmem_limit_bytes=32 << 20),
        cost_estimate=pl.CostEstimate(flops=10**6, bytes_accessed=1 << 20, transcendentals=0),
        name=kernel.__name__,
    )(*args)


def update_kernel(
    info, trailing, col_own, col_oth, er_own, er_oth, across, pay_own, pay_oth,
    f0, i0h, i0l, lp1, f1, i1h, i1l, panels, out, l0t, l1t,
):
    step = pl.program_id(0)
    p0, p1 = info[0], info[1]
    i0 = (i0h[...], i0l[...])
    i1 = (i1h[...], i1l[...])
    ep0 = payload_rows(pay_own, pay_oth, 1)
    ep1 = payload_rows(pay_own, pay_oth, 3)

    def eg(t):
        return across[:, (6 + t) * B : (7 + t) * B]

    @pl.when(step == 0)
    def _():
        for t in range(3):
            cols = slice(t * B, t * B + B)
            c0 = across[:, cols].astype(F32) - dot(ep0, eg(t), 1, 1)
            l0 = dot3(i0, split(c0), 1, 0).astype(BF16)
            l0t[:, cols] = l0
            c1 = across[:, (3 + t) * B : (4 + t) * B].astype(F32) - dot(ep1, eg(t), 1, 1)
            c1 = c1 - dot(lp1[...], l0, 1, 0)
            l1t[:, cols] = dot3(i1, split(c1), 1, 0).astype(BF16)

    tile = info[2] * 3 + step
    er = jnp.concatenate([er_own[...], er_oth[...]], 1)
    c0 = by_core(info, col_own[:, :HALF], col_oth[:, :HALF]) - dot(er, ep0, 1, 1)
    l0 = dot3(split(c0), i0, 1, 1).astype(BF16)
    l0 = jnp.where(tile == p0, f0[...], l0)
    c1 = by_core(info, col_own[:, HALF:], col_oth[:, HALF:]) - dot(er, ep1, 1, 1) - dot(l0, lp1[...], 1, 1)
    l1 = dot3(split(c1), i1, 1, 1).astype(BF16)
    l1 = jnp.where(tile == p1, f1[...], l1)
    l1 = jnp.where(tile == p0, jnp.zeros_like(l1), l1)
    panels[...] = jnp.where(info[4] == 0, l0, l1)
    row_kept = jnp.logical_and(tile != p0, tile != p1)
    for t in range(3):
        cols = slice(t * B, t * B + B)
        col_tile = info[3] * 3 + t
        kept = jnp.logical_and(row_kept, jnp.logical_and(col_tile != p0, col_tile != p1))
        c = trailing[:, cols].astype(F32) - (
            dot(er, eg(t), 1, 1) + dot(l0, l0t[:, cols], 1, 0) + dot(l1, l1t[:, cols], 1, 0)
        )
        out[:, cols] = jnp.where(kept, c, 0.0).astype(BF16)


def update(info, by_rows, whole):
    n = by_rows[0].shape[0]

    def rows(x):
        return pl.BlockSpec((B, x.shape[1]), lambda i, s: (i, 0))

    def all_of(x):
        return pl.BlockSpec(x.shape, lambda i, s: (0, 0))

    out_shape = [jax.ShapeDtypeStruct((n, B), BF16), jax.ShapeDtypeStruct((n, n), BF16)]
    return pl.pallas_call(
        update_kernel,
        out_shape=out_shape,
        grid_spec=pltpu.PrefetchScalarGridSpec(
            num_scalar_prefetch=1,
            grid=(n // B,),
            in_specs=[rows(x) for x in by_rows] + [all_of(x) for x in whole],
            out_specs=[rows(x) for x in out_shape],
            scratch_shapes=[pltpu.VMEM((B, n), BF16)] * 2,
        ),
        compiler_params=pltpu.CompilerParams(vmem_limit_bytes=56 << 20),
        cost_estimate=pl.CostEstimate(flops=25 * 10**9, bytes_accessed=24 << 20, transcendentals=0),
        name="update",
    )(info, *by_rows, *whole)


def tile_start(info, which):
    return pl.multiple_of(lax.rem(info[which], 3) * B, B)


def half_lanes(start, half):
    return pl.ds(pl.multiple_of(start + half * HALF, HALF), HALF)


def run_copies(pairs, sems):
    copies = [pltpu.make_async_copy(a, b, sems.at[i]) for i, (a, b) in enumerate(pairs)]
    for c in copies:
        c.start()
    for c in copies:
        c.wait()


TILE_PARTS = ((0, 0, 0), (1, 0, 2), (1, 1, 4))


def lanes_at(i):
    return pl.ds(i * HALF, HALF)


def send_tiles(info, trailing, out, sems):
    other = 1 - info[4]
    run_copies(
        [
            (
                trailing.at[pl.ds(tile_start(info, i), B), half_lanes(tile_start(info, j), other)],
                out.at[:, lanes_at(k)],
            )
            for k, (i, j, _) in enumerate(TILE_PARTS)
        ],
        sems,
    )


def owner_core(info, which):
    return lax.rem(lax.div(info[which], 3), 2)


def keep_tiles(info, trailing, earlier, got, out, sems):
    copies = [
        pltpu.make_async_copy(earlier.at[pl.ds(tile_start(info, i), B), :], out.at[:, lanes_at(2 * i + 1)], sems.at[i])
        for i in (0, 1)
    ]
    for c in copies:
        c.start()
    for k, (i, j, place) in enumerate(TILE_PARTS):
        mine = pltpu.make_async_copy(
            trailing.at[pl.ds(tile_start(info, i), B), half_lanes(tile_start(info, j), info[4])],
            out.at[:, lanes_at(place)],
            sems.at[2 + k],
        )
        theirs = pltpu.make_async_copy(got.at[:, lanes_at(k)], out.at[:, lanes_at(place)], sems.at[2 + k])
        here = owner_core(info, j) == info[4]
        pl.when(here)(mine.start)
        pl.when(jnp.logical_not(here))(theirs.start)
        copies.append(mine)
    for c in copies:
        c.wait()


def send_columns(info, trailing, out, sems):
    other = 1 - info[4]
    run_copies(
        [(trailing.at[:, half_lanes(tile_start(info, j), other)], out.at[:, lanes_at(j)]) for j in (0, 1)], sems
    )


def keep_columns(info, trailing, got, out, sems):
    copies = []
    for j in (0, 1):
        mine = pltpu.make_async_copy(
            trailing.at[:, half_lanes(tile_start(info, j), info[4])], out.at[:, lanes_at(j)], sems.at[j]
        )
        theirs = pltpu.make_async_copy(got.at[:, lanes_at(j)], out.at[:, lanes_at(j)], sems.at[j])
        here = owner_core(info, j) == info[4]
        pl.when(here)(mine.start)
        pl.when(jnp.logical_not(here))(theirs.start)
        copies.append(mine)
    for c in copies:
        c.wait()


def rows_to_sum(info, trailing, earlier, earlier_other, out, sems):
    n = trailing.shape[1]
    jobs = []
    for j in (0, 1):
        held = lax.div(info[j], 3) == info[2]
        pairs = [(trailing.at[pl.ds(tile_start(info, j), B), :], out.at[:, pl.ds(j * n, n)])]
        jobs.append((held, pairs, j * n))
    held = info[3] == info[2]
    pairs = []
    for t in range(3):
        rows = pl.ds(t * B, B)
        pairs.append((earlier.at[rows, :], out.at[:, pl.ds(2 * n + t * B, HALF)]))
        pairs.append((earlier_other.at[rows, :], out.at[:, pl.ds(2 * n + t * B + HALF, HALF)]))
    jobs.append((held, pairs, 2 * n))
    at = 0
    for held, pairs, start in jobs:
        sem = [sems.at[at + i] for i in range(len(pairs))]
        at += len(pairs)

        @pl.when(held)
        def _():
            copies = [pltpu.make_async_copy(a, b, s) for (a, b), s in zip(pairs, sem)]
            for c in copies:
                c.start()
            for c in copies:
                c.wait()

        @pl.when(jnp.logical_not(held))
        def _():
            out[:, start : start + n] = jnp.zeros((B, n), BF16)


def copy_call(kernel, shape, info, args, count, out_space):
    return pl.pallas_call(
        kernel,
        out_shape=jax.ShapeDtypeStruct(shape, BF16),
        in_specs=[pl.BlockSpec(memory_space=pltpu.SMEM)] + [pl.BlockSpec(memory_space=pl.ANY)] * len(args),
        out_specs=pl.BlockSpec(memory_space=out_space),
        scratch_shapes=[pltpu.SemaphoreType.DMA((count,))],
        compiler_params=pltpu.CompilerParams(vmem_limit_bytes=16 << 20),
        cost_estimate=pl.CostEstimate(flops=10**6, bytes_accessed=1 << 20, transcendentals=0),
        name=kernel.__name__,
    )(info, *args)


barrier = lax.optimization_barrier


def swap(x, axis, mask):
    size = lax.axis_size(axis)
    return lax.ppermute(x, axis, [(i, i ^ mask) for i in range(size)])


def lane_roots(width, parts):
    lane = lax.broadcasted_iota(jnp.int32, (1, width), 1)
    out = jnp.full((1, width), parts[-1][1], jnp.int32)
    for end, root in reversed(parts[:-1]):
        out = jnp.where(lane < end, root, out)
    return out


def ring_sends(chunks, me):
    return tuple(lax.dynamic_index_in_dim(chunks, me ^ k, 0, keepdims=False) for k in (1, 2, 3))


def ring_moves(sent, axis, step):
    return tuple(swap(x, axis, k * step) for x, k in zip(sent, (1, 2, 3)))


def ring_pick(chunks, got, me, root):
    out = lax.dynamic_index_in_dim(chunks, me, 0, keepdims=False)
    for k in (1, 2, 3):
        out = jnp.where((me ^ root) == k, got[k - 1], out)
    return out


def ring_take(chunks, axis, step, me, root):
    return ring_pick(chunks, barrier(ring_moves(barrier(ring_sends(chunks, me)), axis, step)), me, root)


def ring_parts(x, got, me):
    parts = []
    for k in range(4):
        other = me ^ k
        parts.append(
            jnp.where(other == 0, x, jnp.where(other == 1, got[0], jnp.where(other == 2, got[1], got[2])))
        )
    return jnp.concatenate(parts, 0)


def ring_join(x, axis, step, me):
    return ring_parts(x, barrier(ring_moves((x, x, x), axis, step)), me)


def col_spread(x, me, root):
    got = barrier(ring_moves((x, x, x), "col", 1))
    out = x
    for k in (1, 2, 3):
        out = jnp.where(((me ^ root) & 3) == k, got[k - 1], out)
    got = swap(out, "col", 7)
    return jnp.where((me >> 2) != (root >> 2), got, out)


def folded(z):
    return jnp.where(z < 4, z, 7 - z)


def as_one_step(here, f, *args):
    def nothing(*xs):
        return jax.tree.map(lambda o: jnp.zeros(o.shape, o.dtype), jax.eval_shape(f, *xs))

    return lax.cond(here, f, nothing, *args)


def body(trailing, earlier, block_order):
    z = lax.axis_index("col")
    d = lax.axis_index("depth")
    r = lax.axis_index("row")
    g = 2 * z + d
    n = trailing.shape[0]
    count = n // B
    p0, p1 = block_order[0], block_order[1]
    g0, g1 = p0 // count, p1 // count
    z0, z1 = g0 >> 1, g1 >> 1
    x_here, y_here = r >> 2, r & 3
    info = jnp.stack([p0, p1, r, g, d]).astype(jnp.int32)

    earlier_other = swap(earlier, "depth", 1)
    sent = copy_call(send_tiles, (B, 3 * HALF), info, (trailing,), 3, pl.ANY)
    sent, info_b = barrier((sent, info))
    got = swap(sent, "depth", 1)

    share = copy_call(rows_to_sum, (B, 3 * n), info_b, (trailing, earlier, earlier_other), 8, pltpu.VMEM)
    got, share = barrier((got, share))
    across = lax.psum(share, "row")

    pay = copy_call(keep_tiles, (B, 5 * HALF), info, (trailing, earlier, got), 5, pl.ANY)
    width = pay.shape[1]
    row_root = lane_roots(width, [(2 * HALF, g0), (width, g1)])
    col_root = lane_roots(width, [(HALF, z0), (2 * HALF, z), (3 * HALF, z0), (4 * HALF, z), (width, z1)])
    chunks = pay.reshape(4, B // 4, width)
    sent, info_c = barrier((ring_sends(chunks, y_here), info_b))
    moved = ring_moves(sent, "row", 1)

    send = copy_call(send_columns, (n, B), info_c, (trailing,), 2, pl.ANY)
    column = copy_call(keep_columns, (n, B), info_c, (trailing, swap(send, "depth", 1)), 2, pl.ANY)
    column = column.reshape(4, n // 4, B)
    fold = folded(z)
    column_root = lane_roots(B, [(HALF, z0), (B, z1)])
    moved, column_sent = barrier((moved, ring_sends(column, fold)))
    here = p0 >= 0

    def spread(moved):
        out = ring_pick(chunks, moved, y_here, row_root & 3)
        out = ring_take(out.reshape(4, B // 16, width), "row", 4, x_here, row_root >> 2)
        out = col_spread(out, z, col_root)
        out = ring_join(out, "row", 4, x_here)
        out = ring_join(out, "row", 1, y_here)
        return out, swap(out, "depth", 1)

    def factors(moved, column_sent):
        column_got = ring_moves(column_sent, "col", 1)
        pay, other = as_one_step(here, spread, moved)
        pay, other, column_got = barrier((pay, other, column_got))
        part = ring_pick(column, column_got, fold, folded(column_root))
        pay, part = barrier((pay, part))
        column_got = swap(part, "col", 7)
        state = tuple(tile_call(first_factor, [NARROW] * 4 + [WIDE], 2, (pay, other), info))
        state, column_got = barrier((state, column_got))
        f0, i0h, i0l, lp1, work = state
        part = jnp.where((z >> 2) != (column_root >> 2), column_got, part)
        work, part = barrier((work, part))
        column_got = ring_moves((part,) * 3, "col", 1)
        state = tuple(tile_call(second_factor, [NARROW] * 3, 2, (work,)))
        state, column_got = barrier((state, column_got))
        f1, i1h, i1l = state
        whole = ring_parts(part, column_got, fold)
        return whole, swap(whole, "depth", 1), pay, other, f0, i0h, i0l, lp1, f1, i1h, i1l

    column, column_other, *rest = as_one_step(here, factors, moved, column_sent)
    panels, out = update(
        info,
        [trailing, column, column_other, earlier, earlier_other],
        [across, *rest],
    )
    return panels, out


def solution(mesh):
    placed = (P("row", ("col", "depth")), P("row", "depth"), P())
    return jax.shard_map(
        body,
        mesh=mesh,
        in_specs=placed,
        out_specs=(P("row", "depth"), P("row", ("col", "depth"))),
        check_vma=False,
    )
```

```python
import jax
import jax.numpy as jnp
from jax import lax
from jax.experimental import pallas as pl
from jax.experimental.pallas import tpu as pltpu
from jax.sharding import PartitionSpec as P

B = 512
F32 = jnp.float32
BF16 = jnp.bfloat16
HIGHEST = lax.Precision.HIGHEST


def pivot_block(d):
    n = 8
    d = [row[:] for row in d]
    low = [[None] * n for _ in range(n)]
    inv = [None] * n
    diag = [None] * n
    for j in range(0, n, 2):
        a, b, c = d[j][j], d[j + 1][j], d[j + 1][j + 1]
        det = a * c - b * b
        inv[j] = 1.0 / a
        inv_det = 1.0 / det
        inv[j + 1] = a * inv_det
        diag[j] = a
        diag[j + 1] = det * inv[j]
        low[j + 1][j] = b * inv[j]
        for i in range(j + 2, n):
            low[i][j] = d[i][j] * inv[j]
            low[i][j + 1] = (a * d[i][j + 1] - b * d[i][j]) * inv_det
        for i in range(j + 2, n):
            first = (c * d[i][j] - b * d[i][j + 1]) * inv_det
            for k in range(j + 2, i + 1):
                d[i][k] = d[i][k] - (first * d[k][j] + low[i][j + 1] * d[k][j + 1])
    return low, inv, diag


def chol_128(work, upper, base):
    lane = lax.broadcasted_iota(jnp.int32, (8, 128), 1)
    blocks = [work[base + 8 * m : base + 8 * m + 8, base : base + 128] for m in range(16)]

    def over_lanes(x, k):
        return jnp.broadcast_to(x[:, k : k + 1], (8, 128))

    def over_rows(x, k):
        return jnp.broadcast_to(x[k : k + 1, :], (8, 128))

    for q in range(16):
        o = 8 * q
        pivot = blocks[q]
        cols = [over_lanes(pivot, o + j) for j in range(8)]
        entries = [[over_rows(cols[j], i) if j <= i else None for j in range(8)] for i in range(8)]
        low, inv, diag = pivot_block(entries)
        inside = (lane >= o) & (lane < o + 8)
        solved = []
        for j in range(8):
            u = jnp.where(inside, jnp.where(lane == o + j, 1.0, 0.0), over_rows(pivot, j))
            for i in range(j):
                u = u - low[j][i] * solved[i]
            solved.append(u)
        if q < 15:
            back = [None] * 8
            for i in reversed(range(8)):
                g = solved[i] * inv[i]
                for j in range(i + 1, 8):
                    g = g - low[j][i] * back[j]
                back[i] = g
            for m in range(q + 1, 16):
                x = blocks[m]
                acc = jnp.where(inside, 0.0, x)
                for i in range(8):
                    acc = acc - over_lanes(x, o + i) * back[i]
                blocks[m] = acc
        for j in range(8):
            scale = lax.rsqrt(diag[j])
            root = diag[j] * scale
            row = solved[j] * scale
            up = jnp.where(lane < o + 8, 0.0, row)
            up = jnp.where(lane == o + j, root, up)
            for i in range(j + 1, 8):
                up = jnp.where(lane == o + i, low[i][j] * root, up)
            upper[base + o + j : base + o + j + 1, base : base + 128] = up[0:1]
            work[base + o + j : base + o + j + 1, base : base + 128] = jnp.where(lane <= o + j, row, 0.0)[0:1]


def dot(a, b, ca, cb, precision=None):
    return lax.dot_general(a, b, (((ca,), (cb,)), ((), ())), precision=precision, preferred_element_type=F32)


def chol_strips(work, upper, strips):
    for b in strips:
        o = 128 * b
        e = o + 128
        chol_128(work, upper, o)
        inv = work[o:e, o:e]
        if b > 0:
            work[o:e, 0:o] = dot(inv, work[o:e, 0:o], 1, 0, HIGHEST)
            upper[o:e, 0:o] = jnp.zeros((128, o), F32)
        if b < 3:
            up = dot(inv, work[o:e, e:B], 1, 0, HIGHEST)
            upper[o:e, e:B] = up
            work[o:e, e:B] = jnp.zeros_like(up)
            work[e:B, o:e] = jnp.zeros((B - e, 128), F32)
            work[e:B, 0:e] = work[e:B, 0:e] - dot(up, work[o:e, 0:e], 0, 0, HIGHEST)
            work[e:B, e:B] = work[e:B, e:B] - dot(up, up, 0, 0, HIGHEST)


def split(x):
    hi = x.astype(BF16)
    return hi, (x - hi.astype(F32)).astype(BF16)


def dot3(a, b, ca, cb):
    return dot(a[0], b[0], ca, cb) + (dot(a[0], b[1], ca, cb) + dot(a[1], b[0], ca, cb))


def symmetric(x):
    return 0.5 * (x + x.T)


def by_core(info, own, other):
    first = info[4] == 0
    own, other = own.astype(F32), other.astype(F32)
    return jnp.concatenate([jnp.where(first, own, other), jnp.where(first, other, own)], 1)


HALF = B // 2


def part(own, other, index):
    lanes = slice(index * HALF, index * HALF + HALF)
    return own[:, lanes], other[:, lanes]


def tile_of(info, own, other, index):
    return by_core(info, *part(own, other, index))


def rows_of(own, other, index):
    return jnp.concatenate(part(own, other, index), 1)


def finish(work, upper, f, ih, il):
    f[...] = upper[...].T.astype(BF16)
    h, l = split(work[...])
    ih[...] = h
    il[...] = l


def first_open(info, own, other, work, upper):
    ep0 = rows_of(own, other, 1)
    work[...] = symmetric(tile_of(info, own, other, 0) - dot(ep0, ep0, 1, 1))
    chol_strips(work, upper, (0, 1))


def first_close(work_in, upper_in, f, ih, il, work, upper):
    work[...] = work_in[...]
    upper[0:HALF] = upper_in[0:HALF]
    chol_strips(work, upper, (2, 3))
    finish(work, upper, f, ih, il)


def second_factor(info, own, other, own2, other2, i0h, i0l, lp, f, ih, il, work, upper):
    ep0 = rows_of(own, other, 1)
    ep1 = rows_of(own2, other2, 2)
    c10 = tile_of(info, own2, other2, 0) - dot(ep1, ep0, 1, 1)
    lp[...] = dot3(split(c10), (i0h[...], i0l[...]), 1, 1).astype(BF16)
    c11 = tile_of(info, own2, other2, 1) - dot(ep1, ep1, 1, 1) - dot(lp[...], lp[...], 1, 1)
    work[...] = symmetric(c11)
    chol_strips(work, upper, (0, 1, 2, 3))
    finish(work, upper, f, ih, il)


WIDE = jax.ShapeDtypeStruct((B, B), F32)
NARROW = jax.ShapeDtypeStruct((B, B), BF16)


def tile_call(kernel, out_shape, scratch, args, info=None):
    def spec(_):
        return pl.BlockSpec(memory_space=pltpu.VMEM)

    specs = [spec(a) for a in args]
    if info is not None:
        specs = [pl.BlockSpec(memory_space=pltpu.SMEM)] + specs
        args = [info] + list(args)
    return pl.pallas_call(
        kernel,
        out_shape=out_shape,
        in_specs=specs,
        out_specs=[spec(a) for a in out_shape],
        scratch_shapes=[pltpu.VMEM((B, B), F32)] * scratch,
        compiler_params=pltpu.CompilerParams(vmem_limit_bytes=32 << 20),
        cost_estimate=pl.CostEstimate(flops=10**6, bytes_accessed=1 << 20, transcendentals=0),
        name=kernel.__name__,
    )(*args)


def update_kernel(
    info, trailing, col_own, col_oth, er_own, er_oth, across, pay_own, pay_oth, pay2_own, pay2_oth,
    f0, i0h, i0l, lp1, f1, i1h, i1l, panels, out, l0t, l1t,
):
    step = pl.program_id(0)
    p0, p1 = info[0], info[1]
    i0 = (i0h[...], i0l[...])
    i1 = (i1h[...], i1l[...])
    ep0 = rows_of(pay_own, pay_oth, 1)
    ep1 = rows_of(pay2_own, pay2_oth, 2)

    def eg(t):
        return across[:, (6 + t) * B : (7 + t) * B]

    @pl.when(step == 0)
    def _():
        for t in range(3):
            cols = slice(t * B, t * B + B)
            c0 = across[:, cols].astype(F32) - dot(ep0, eg(t), 1, 1)
            l0 = dot3(i0, split(c0), 1, 0).astype(BF16)
            l0t[:, cols] = l0
            c1 = across[:, (3 + t) * B : (4 + t) * B].astype(F32) - dot(ep1, eg(t), 1, 1)
            c1 = c1 - dot(lp1[...], l0, 1, 0)
            l1t[:, cols] = dot3(i1, split(c1), 1, 0).astype(BF16)

    tile = info[2] * 3 + step
    er = jnp.concatenate([er_own[...], er_oth[...]], 1)
    c0 = by_core(info, col_own[:, :HALF], col_oth[:, :HALF]) - dot(er, ep0, 1, 1)
    l0 = dot3(split(c0), i0, 1, 1).astype(BF16)
    l0 = jnp.where(tile == p0, f0[...], l0)
    c1 = by_core(info, col_own[:, HALF:], col_oth[:, HALF:]) - dot(er, ep1, 1, 1) - dot(l0, lp1[...], 1, 1)
    l1 = dot3(split(c1), i1, 1, 1).astype(BF16)
    l1 = jnp.where(tile == p1, f1[...], l1)
    l1 = jnp.where(tile == p0, jnp.zeros_like(l1), l1)
    panels[...] = jnp.where(info[4] == 0, l0, l1)
    row_kept = jnp.logical_and(tile != p0, tile != p1)
    for t in range(3):
        cols = slice(t * B, t * B + B)
        col_tile = info[3] * 3 + t
        kept = jnp.logical_and(row_kept, jnp.logical_and(col_tile != p0, col_tile != p1))
        c = trailing[:, cols].astype(F32) - (
            dot(er, eg(t), 1, 1) + dot(l0, l0t[:, cols], 1, 0) + dot(l1, l1t[:, cols], 1, 0)
        )
        out[:, cols] = jnp.where(kept, c, 0.0).astype(BF16)


def update(info, by_rows, whole):
    n = by_rows[0].shape[0]

    def rows(x):
        return pl.BlockSpec((B, x.shape[1]), lambda i, s: (i, 0))

    def all_of(x):
        return pl.BlockSpec(x.shape, lambda i, s: (0, 0))

    out_shape = [jax.ShapeDtypeStruct((n, B), BF16), jax.ShapeDtypeStruct((n, n), BF16)]
    return pl.pallas_call(
        update_kernel,
        out_shape=out_shape,
        grid_spec=pltpu.PrefetchScalarGridSpec(
            num_scalar_prefetch=1,
            grid=(n // B,),
            in_specs=[rows(x) for x in by_rows] + [all_of(x) for x in whole],
            out_specs=[rows(x) for x in out_shape],
            scratch_shapes=[pltpu.VMEM((B, n), BF16)] * 2,
        ),
        compiler_params=pltpu.CompilerParams(vmem_limit_bytes=56 << 20),
        cost_estimate=pl.CostEstimate(flops=25 * 10**9, bytes_accessed=24 << 20, transcendentals=0),
        name="update",
    )(info, *by_rows, *whole)


def tile_start(info, which):
    return pl.multiple_of(lax.rem(info[which], 3) * B, B)


def half_lanes(start, half):
    return pl.ds(pl.multiple_of(start + half * HALF, HALF), HALF)


def run_copies(pairs, sems):
    copies = [pltpu.make_async_copy(a, b, sems.at[i]) for i, (a, b) in enumerate(pairs)]
    for c in copies:
        c.start()
    for c in copies:
        c.wait()


TILE_PARTS = ((0, 0, 0, 0), (1, 0, 1, 0), (1, 1, 1, 1))


def lanes_at(i):
    return pl.ds(i * HALF, HALF)


def send_tiles(info, trailing, out, sems):
    other = 1 - info[4]
    run_copies(
        [
            (
                trailing.at[pl.ds(tile_start(info, i), B), half_lanes(tile_start(info, j), other)],
                out.at[:, lanes_at(k)],
            )
            for k, (i, j, _, _) in enumerate(TILE_PARTS)
        ],
        sems,
    )


def owner_core(info, which):
    return lax.rem(lax.div(info[which], 3), 2)


def keep_tiles(info, trailing, earlier, got, pay, pay2, sems):
    copies = [
        pltpu.make_async_copy(earlier.at[pl.ds(tile_start(info, i), B), :], out.at[:, lanes_at(1 + i)], sems.at[i])
        for i, out in ((0, pay), (1, pay2))
    ]
    for c in copies:
        c.start()
    for k, (i, j, which, place) in enumerate(TILE_PARTS):
        out = (pay, pay2)[which].at[:, lanes_at(place)]
        mine = pltpu.make_async_copy(
            trailing.at[pl.ds(tile_start(info, i), B), half_lanes(tile_start(info, j), info[4])], out, sems.at[2 + k]
        )
        theirs = pltpu.make_async_copy(got.at[:, lanes_at(k)], out, sems.at[2 + k])
        here = owner_core(info, j) == info[4]
        pl.when(here)(mine.start)
        pl.when(jnp.logical_not(here))(theirs.start)
        copies.append(mine)
    for c in copies:
        c.wait()


def send_columns(info, trailing, out, sems):
    other = 1 - info[4]
    run_copies(
        [(trailing.at[:, half_lanes(tile_start(info, j), other)], out.at[:, lanes_at(j)]) for j in (0, 1)], sems
    )


def keep_columns(info, trailing, got, out, sems):
    copies = []
    for j in (0, 1):
        mine = pltpu.make_async_copy(
            trailing.at[:, half_lanes(tile_start(info, j), info[4])], out.at[:, lanes_at(j)], sems.at[j]
        )
        theirs = pltpu.make_async_copy(got.at[:, lanes_at(j)], out.at[:, lanes_at(j)], sems.at[j])
        here = owner_core(info, j) == info[4]
        pl.when(here)(mine.start)
        pl.when(jnp.logical_not(here))(theirs.start)
        copies.append(mine)
    for c in copies:
        c.wait()


def rows_to_sum(info, trailing, earlier, earlier_other, out, sems):
    n = trailing.shape[1]
    jobs = []
    for j in (0, 1):
        held = lax.div(info[j], 3) == info[2]
        pairs = [(trailing.at[pl.ds(tile_start(info, j), B), :], out.at[:, pl.ds(j * n, n)])]
        jobs.append((held, pairs, j * n))
    held = info[3] == info[2]
    pairs = []
    for t in range(3):
        rows = pl.ds(t * B, B)
        pairs.append((earlier.at[rows, :], out.at[:, pl.ds(2 * n + t * B, HALF)]))
        pairs.append((earlier_other.at[rows, :], out.at[:, pl.ds(2 * n + t * B + HALF, HALF)]))
    jobs.append((held, pairs, 2 * n))
    at = 0
    for held, pairs, start in jobs:
        sem = [sems.at[at + i] for i in range(len(pairs))]
        at += len(pairs)

        @pl.when(held)
        def _():
            copies = [pltpu.make_async_copy(a, b, s) for (a, b), s in zip(pairs, sem)]
            for c in copies:
                c.start()
            for c in copies:
                c.wait()

        @pl.when(jnp.logical_not(held))
        def _():
            out[:, start : start + n] = jnp.zeros((B, n), BF16)


def copy_call(kernel, shapes, info, args, count, out_space=pl.ANY):
    return pl.pallas_call(
        kernel,
        out_shape=[jax.ShapeDtypeStruct(shape, BF16) for shape in shapes],
        in_specs=[pl.BlockSpec(memory_space=pltpu.SMEM)] + [pl.BlockSpec(memory_space=pl.ANY)] * len(args),
        out_specs=[pl.BlockSpec(memory_space=out_space)] * len(shapes),
        scratch_shapes=[pltpu.SemaphoreType.DMA((count,))],
        compiler_params=pltpu.CompilerParams(vmem_limit_bytes=56 << 20),
        cost_estimate=pl.CostEstimate(flops=10**6, bytes_accessed=1 << 20, transcendentals=0),
        name=kernel.__name__,
    )(info, *args)


barrier = lax.optimization_barrier


def swap(x, axis, mask):
    size = lax.axis_size(axis)
    return lax.ppermute(x, axis, [(i, i ^ mask) for i in range(size)])


def lane_roots(width, parts):
    lane = lax.broadcasted_iota(jnp.int32, (1, width), 1)
    out = jnp.full((1, width), parts[-1][1], jnp.int32)
    for end, root in reversed(parts[:-1]):
        out = jnp.where(lane < end, root, out)
    return out


def ring_sends(chunks, me):
    return tuple(lax.dynamic_index_in_dim(chunks, me ^ k, 0, keepdims=False) for k in (1, 2, 3))


def ring_moves(sent, axis, step):
    return tuple(swap(x, axis, k * step) for x, k in zip(sent, (1, 2, 3)))


def ring_pick(chunks, got, me, root):
    out = lax.dynamic_index_in_dim(chunks, me, 0, keepdims=False)
    for k in (1, 2, 3):
        out = jnp.where((me ^ root) == k, got[k - 1], out)
    return out


def ring_parts(x, got, me):
    parts = []
    for k in range(4):
        other = me ^ k
        parts.append(
            jnp.where(other == 0, x, jnp.where(other == 1, got[0], jnp.where(other == 2, got[1], got[2])))
        )
    return jnp.concatenate(parts, 0)


def gray(x, bit):
    return ((x >> bit) ^ (x >> (bit + 1))) & 1


def col_pick(x, got, me, root):
    for k in (1, 2, 3):
        x = jnp.where(((me ^ root) & 3) == k, got[k - 1], x)
    return x


def halves(x, bit):
    n = x.shape[0] // 2
    return lax.dynamic_slice_in_dim(x, (1 - bit) * n, n, 0), lax.dynamic_slice_in_dim(x, bit * n, n, 0)


def joined(x, got, bit):
    return jnp.where(bit == 0, jnp.concatenate([x, got], 0), jnp.concatenate([got, x], 0))


def as_one_step(here, f, *args):
    def nothing(*xs):
        return jax.tree.map(lambda o: jnp.zeros(o.shape, o.dtype), jax.eval_shape(f, *xs))

    return lax.cond(here, f, nothing, *args)


def body(trailing, earlier, block_order):
    z = lax.axis_index("col")
    d = lax.axis_index("depth")
    r = lax.axis_index("row")
    g = 2 * z + d
    n = trailing.shape[0]
    count = n // B
    p0, p1 = block_order[0], block_order[1]
    g0, g1 = p0 // count, p1 // count
    z0, z1 = g0 >> 1, g1 >> 1
    x_here, y_here = r >> 2, r & 3
    info = jnp.stack([p0, p1, r, g, d]).astype(jnp.int32)

    earlier_other = swap(earlier, "depth", 1)
    (sent,) = copy_call(send_tiles, [(B, 3 * HALF)], info, (trailing,), 3)
    sent, info_b = barrier((sent, info))
    got = swap(sent, "depth", 1)

    (share,) = copy_call(rows_to_sum, [(B, 3 * n)], info_b, (trailing, earlier, earlier_other), 8, pltpu.VMEM)
    got, share = barrier((got, share))
    across = lax.psum(share, "row")

    pay, pay2 = copy_call(keep_tiles, [(B, 2 * HALF), (B, 3 * HALF)], info, (trailing, earlier, got), 5)
    chunks = pay.reshape(4, B // 4, 2 * HALF)
    sent, info_c = barrier((ring_sends(chunks, y_here), info_b))
    moved = ring_moves(sent, "row", 1)

    (send,) = copy_call(send_columns, [(n, B)], info_c, (trailing,), 2)
    (column,) = copy_call(keep_columns, [(n, B)], info_c, (trailing, swap(send, "depth", 1)), 2)
    column_root = lane_roots(B, [(HALF, z0), (B, z1)])
    b1, b2, b3 = gray(z, 0), gray(z, 1), z >> 2
    away, kept = halves(column, b1)
    moved, away = barrier((moved, away))
    here = p0 >= 0

    def scatter(moved):
        q = ring_pick(chunks, moved, y_here, g0 & 3)
        first, second = q.reshape(4, B // 16, 2 * HALF), pay2.reshape(4, B // 4, 3 * HALF)
        sent = barrier((ring_sends(first, x_here), ring_sends(second, y_here)))
        got = barrier((ring_moves(sent[0], "row", 4), ring_moves(sent[1], "row", 1)))
        q = ring_pick(first, got[0], x_here, g0 >> 2)
        q2 = ring_pick(second, got[1], y_here, g1 & 3)
        second = q2.reshape(4, B // 16, 3 * HALF)
        tile, sent = barrier((q[:, :HALF], ring_sends(second, x_here)))
        got = barrier((ring_moves((tile,) * 3, "col", 1), ring_moves(sent, "row", 4)))
        return q[:, HALF:], col_pick(tile, got[0], z, z0), ring_pick(second, got[1], x_here, g1 >> 2)

    def gather(rows, tile, q2):
        tiles = q2[:, : 2 * HALF]
        tiles_root = lane_roots(2 * HALF, [(HALF, z0), (2 * HALF, z1)])
        tile, tiles = barrier((tile, tiles))
        got = barrier((swap(tile, "col", 7), ring_moves((tiles,) * 3, "col", 1)))
        tile = jnp.where(b3 != z0 >> 2, got[0], tile)
        tiles = col_pick(tiles, got[1], z, tiles_root)
        q, tiles = barrier((jnp.concatenate([tile, rows], 1), tiles))
        got = barrier((ring_moves((q,) * 3, "row", 4), swap(tiles, "col", 7)))
        q = ring_parts(q, got[0], x_here)
        tiles = jnp.where(b3 != tiles_root >> 2, got[1], tiles)
        q, q2 = barrier((q, jnp.concatenate([tiles, q2[:, 2 * HALF :]], 1)))
        got = barrier((ring_moves((q,) * 3, "row", 1), ring_moves((q2,) * 3, "row", 4)))
        q = ring_parts(q, got[0], y_here)
        return q, swap(q, "depth", 1), ring_parts(q2, got[1], x_here)

    def factors(moved, away):
        got = swap(away, "col", 1)
        state = as_one_step(here, scatter, moved)
        state, got = barrier((state, got))
        away, kept2 = halves(jnp.where(gray(column_root, 0) != b1, got, kept), b2)
        state, away = barrier((state, away))
        got = swap(away, "col", 3)
        state = as_one_step(here, gather, *state)
        state, got = barrier((state, got))
        pay, other, q2 = state
        x = jnp.where(gray(column_root, 1) != b2, got, kept2)
        pay, q2, x = barrier((pay, q2, x))
        got2 = ring_moves((q2,) * 3, "row", 1)
        got = swap(x, "col", 7)
        state = tuple(tile_call(first_open, [WIDE] * 2, 0, (pay, other), info))
        state, got, got2 = barrier((state, got, got2))
        x = jnp.where(b3 != column_root >> 2, got, x)
        state, x, pay2 = barrier((state, x, ring_parts(q2, got2, y_here)))
        got2 = swap(pay2, "depth", 1)
        got = swap(x, "col", 3)
        state = tuple(tile_call(first_close, [NARROW] * 3, 2, state))
        state, got, other2 = barrier((state, got, got2))
        f0, i0h, i0l = state
        i0h, x = barrier((i0h, joined(x, got, b2)))
        got = swap(x, "col", 1)
        state = tuple(tile_call(second_factor, [NARROW] * 4, 2, (pay, other, pay2, other2, i0h, i0l), info))
        state, got = barrier((state, got))
        lp1, f1, i1h, i1l = state
        whole = joined(x, got, b1)
        return whole, swap(whole, "depth", 1), pay, other, pay2, other2, f0, i0h, i0l, lp1, f1, i1h, i1l

    column, column_other, *rest = as_one_step(here, factors, moved, away)
    panels, out = update(
        info, [trailing, column, column_other, earlier, earlier_other], [across, *rest]
    )
    return panels, out


def solution(mesh):
    placed = (P("row", ("col", "depth")), P("row", "depth"), P())
    return jax.shard_map(
        body,
        mesh=mesh,
        in_specs=placed,
        out_specs=(P("row", "depth"), P("row", ("col", "depth"))),
        check_vma=False,
    )
```

```python
import jax
import jax.numpy as jnp
from jax import lax
from jax.experimental import pallas as pl
from jax.experimental.pallas import tpu as pltpu
from jax.sharding import PartitionSpec as P

B = 512
F32 = jnp.float32
BF16 = jnp.bfloat16
HIGHEST = lax.Precision.HIGHEST


def pivot_block(d):
    n = 8
    d = [row[:] for row in d]
    low = [[None] * n for _ in range(n)]
    inv = [None] * n
    diag = [None] * n
    for j in range(0, n, 2):
        a, b, c = d[j][j], d[j + 1][j], d[j + 1][j + 1]
        det = a * c - b * b
        inv[j] = 1.0 / a
        inv_det = 1.0 / det
        inv[j + 1] = a * inv_det
        diag[j] = a
        diag[j + 1] = det * inv[j]
        low[j + 1][j] = b * inv[j]
        for i in range(j + 2, n):
            low[i][j] = d[i][j] * inv[j]
            low[i][j + 1] = (a * d[i][j + 1] - b * d[i][j]) * inv_det
        for i in range(j + 2, n):
            first = (c * d[i][j] - b * d[i][j + 1]) * inv_det
            for k in range(j + 2, i + 1):
                d[i][k] = d[i][k] - (first * d[k][j] + low[i][j + 1] * d[k][j + 1])
    return low, inv, diag


def chol_128(work, upper, base):
    lane = lax.broadcasted_iota(jnp.int32, (8, 128), 1)
    blocks = [work[base + 8 * m : base + 8 * m + 8, base : base + 128] for m in range(16)]

    def over_lanes(x, k):
        return jnp.broadcast_to(x[:, k : k + 1], (8, 128))

    def over_rows(x, k):
        return jnp.broadcast_to(x[k : k + 1, :], (8, 128))

    for q in range(16):
        o = 8 * q
        pivot = blocks[q]
        cols = [over_lanes(pivot, o + j) for j in range(8)]
        entries = [[over_rows(cols[j], i) if j <= i else None for j in range(8)] for i in range(8)]
        low, inv, diag = pivot_block(entries)
        inside = (lane >= o) & (lane < o + 8)
        solved = []
        for j in range(8):
            u = jnp.where(inside, jnp.where(lane == o + j, 1.0, 0.0), over_rows(pivot, j))
            for i in range(j):
                u = u - low[j][i] * solved[i]
            solved.append(u)
        if q < 15:
            back = [None] * 8
            for i in reversed(range(8)):
                g = solved[i] * inv[i]
                for j in range(i + 1, 8):
                    g = g - low[j][i] * back[j]
                back[i] = g
            for m in range(q + 1, 16):
                x = blocks[m]
                acc = jnp.where(inside, 0.0, x)
                for i in range(8):
                    acc = acc - over_lanes(x, o + i) * back[i]
                blocks[m] = acc
        for j in range(8):
            scale = lax.rsqrt(diag[j])
            root = diag[j] * scale
            row = solved[j] * scale
            up = jnp.where(lane < o + 8, 0.0, row)
            up = jnp.where(lane == o + j, root, up)
            for i in range(j + 1, 8):
                up = jnp.where(lane == o + i, low[i][j] * root, up)
            upper[base + o + j : base + o + j + 1, base : base + 128] = up[0:1]
            work[base + o + j : base + o + j + 1, base : base + 128] = jnp.where(lane <= o + j, row, 0.0)[0:1]


def dot(a, b, ca, cb, precision=None):
    return lax.dot_general(a, b, (((ca,), (cb,)), ((), ())), precision=precision, preferred_element_type=F32)


def chol_strips(work, upper, strips):
    for b in strips:
        o = 128 * b
        e = o + 128
        chol_128(work, upper, o)
        inv = work[o:e, o:e]
        if b > 0:
            work[o:e, 0:o] = dot(inv, work[o:e, 0:o], 1, 0, HIGHEST)
            upper[o:e, 0:o] = jnp.zeros((128, o), F32)
        if b < 3:
            up = dot(inv, work[o:e, e:B], 1, 0, HIGHEST)
            upper[o:e, e:B] = up
            work[o:e, e:B] = jnp.zeros_like(up)
            work[e:B, o:e] = jnp.zeros((B - e, 128), F32)
            work[e:B, 0:e] = work[e:B, 0:e] - dot(up, work[o:e, 0:e], 0, 0, HIGHEST)
            work[e:B, e:B] = work[e:B, e:B] - dot(up, up, 0, 0, HIGHEST)


def split(x):
    hi = x.astype(BF16)
    return hi, (x - hi.astype(F32)).astype(BF16)


def dot3(a, b, ca, cb):
    return dot(a[0], b[0], ca, cb) + (dot(a[0], b[1], ca, cb) + dot(a[1], b[0], ca, cb))


def times_lower_t(x, low):
    h = B // 2
    left = dot3([v[:, :h] for v in x], [v[:h, :h] for v in low], 1, 1)
    return jnp.concatenate([left, dot3(x, [v[h:] for v in low], 1, 1)], 1)


def lower_times(low, x):
    h = B // 2
    top = dot3([v[:h, :h] for v in low], [v[:h] for v in x], 1, 0)
    return jnp.concatenate([top, dot3([v[h:] for v in low], x, 1, 0)], 0)


def symmetric(x):
    return 0.5 * (x + x.T)


def by_core(info, own, other):
    first = info[4] == 0
    own, other = own.astype(F32), other.astype(F32)
    return jnp.concatenate([jnp.where(first, own, other), jnp.where(first, other, own)], 1)


HALF = B // 2


def payload_part(own, other, index):
    lanes = slice(index * HALF, index * HALF + HALF)
    return own[:, lanes], other[:, lanes]


def payload_tile(info, own, other, index):
    return by_core(info, *payload_part(own, other, index))


def payload_rows(own, other, index):
    return jnp.concatenate(payload_part(own, other, index), 1)


def finish(work, upper, f, ih, il):
    f[...] = upper[...].T.astype(BF16)
    h, l = split(work[...])
    ih[...] = h
    il[...] = l


def first_factor(info, own, other, f, ih, il, lp, next_work, work, upper):
    ep0 = payload_rows(own, other, 1)
    ep1 = payload_rows(own, other, 3)
    work[...] = symmetric(payload_tile(info, own, other, 0) - dot(ep0, ep0, 1, 1))
    chol_strips(work, upper, (0, 1, 2, 3))
    finish(work, upper, f, ih, il)
    c10 = payload_tile(info, own, other, 2) - dot(ep1, ep0, 1, 1)
    lp[...] = dot3(split(c10), (ih[...], il[...]), 1, 1).astype(BF16)
    c11 = payload_tile(info, own, other, 4) - dot(ep1, ep1, 1, 1) - dot(lp[...], lp[...], 1, 1)
    next_work[...] = symmetric(c11)


def second_factor(work_in, f, ih, il, work, upper):
    work[...] = work_in[...]
    chol_strips(work, upper, (0, 1, 2, 3))
    finish(work, upper, f, ih, il)


WIDE = jax.ShapeDtypeStruct((B, B), F32)
NARROW = jax.ShapeDtypeStruct((B, B), BF16)


def tile_call(kernel, out_shape, scratch, args, info=None):
    def spec(_):
        return pl.BlockSpec(memory_space=pltpu.VMEM)

    specs = [spec(a) for a in args]
    if info is not None:
        specs = [pl.BlockSpec(memory_space=pltpu.SMEM)] + specs
        args = [info] + list(args)
    return pl.pallas_call(
        kernel,
        out_shape=out_shape,
        in_specs=specs,
        out_specs=[spec(a) for a in out_shape],
        scratch_shapes=[pltpu.VMEM((B, B), F32)] * scratch,
        compiler_params=pltpu.CompilerParams(vmem_limit_bytes=32 << 20),
        cost_estimate=pl.CostEstimate(flops=10**6, bytes_accessed=1 << 20, transcendentals=0),
        name=kernel.__name__,
    )(*args)


def update_kernel(
    info, trailing, col_own, col_oth, er_own, er_oth, across, pay_own, pay_oth,
    f0, i0h, i0l, lp1, f1, i1h, i1l, panels, out, l0t, l1t,
):
    step = pl.program_id(0)
    p0, p1 = info[0], info[1]
    i0 = (i0h[...], i0l[...])
    i1 = (i1h[...], i1l[...])
    ep0 = payload_rows(pay_own, pay_oth, 1)
    ep1 = payload_rows(pay_own, pay_oth, 3)

    def eg(t):
        return across[:, (6 + t) * B : (7 + t) * B]

    @pl.when(step == 0)
    def _():
        for t in range(3):
            cols = slice(t * B, t * B + B)
            c0 = across[:, cols].astype(F32) - dot(ep0, eg(t), 1, 1)
            l0 = lower_times(i0, split(c0)).astype(BF16)
            l0t[:, cols] = l0
            c1 = across[:, (3 + t) * B : (4 + t) * B].astype(F32) - dot(ep1, eg(t), 1, 1)
            c1 = c1 - dot(lp1[...], l0, 1, 0)
            l1t[:, cols] = lower_times(i1, split(c1)).astype(BF16)

    tile = info[2] * 3 + step
    er = jnp.concatenate([er_own[...], er_oth[...]], 1)
    c0 = by_core(info, col_own[:, :HALF], col_oth[:, :HALF]) - dot(er, ep0, 1, 1)
    l0 = times_lower_t(split(c0), i0).astype(BF16)
    l0 = jnp.where(tile == p0, f0[...], l0)
    c1 = by_core(info, col_own[:, HALF:], col_oth[:, HALF:]) - dot(er, ep1, 1, 1) - dot(l0, lp1[...], 1, 1)
    l1 = times_lower_t(split(c1), i1).astype(BF16)
    l1 = jnp.where(tile == p1, f1[...], l1)
    l1 = jnp.where(tile == p0, jnp.zeros_like(l1), l1)
    panels[...] = jnp.where(info[4] == 0, l0, l1)
    row_kept = jnp.logical_and(tile != p0, tile != p1)
    for t in range(3):
        cols = slice(t * B, t * B + B)
        col_tile = info[3] * 3 + t
        kept = jnp.logical_and(row_kept, jnp.logical_and(col_tile != p0, col_tile != p1))
        c = trailing[:, cols].astype(F32) - (
            dot(er, eg(t), 1, 1) + dot(l0, l0t[:, cols], 1, 0) + dot(l1, l1t[:, cols], 1, 0)
        )
        out[:, cols] = jnp.where(kept, c, 0.0).astype(BF16)


def update(info, by_rows, whole):
    n = by_rows[0].shape[0]

    def rows(x):
        return pl.BlockSpec((B, x.shape[1]), lambda i, s: (i, 0))

    def all_of(x):
        return pl.BlockSpec(x.shape, lambda i, s: (0, 0))

    out_shape = [jax.ShapeDtypeStruct((n, B), BF16), jax.ShapeDtypeStruct((n, n), BF16)]
    return pl.pallas_call(
        update_kernel,
        out_shape=out_shape,
        grid_spec=pltpu.PrefetchScalarGridSpec(
            num_scalar_prefetch=1,
            grid=(n // B,),
            in_specs=[rows(x) for x in by_rows] + [all_of(x) for x in whole],
            out_specs=[rows(x) for x in out_shape],
            scratch_shapes=[pltpu.VMEM((B, n), BF16)] * 2,
        ),
        compiler_params=pltpu.CompilerParams(vmem_limit_bytes=56 << 20),
        cost_estimate=pl.CostEstimate(flops=25 * 10**9, bytes_accessed=24 << 20, transcendentals=0),
        name="update",
    )(info, *by_rows, *whole)


def tile_start(info, which):
    return pl.multiple_of(lax.rem(info[which], 3) * B, B)


def half_lanes(start, half):
    return pl.ds(pl.multiple_of(start + half * HALF, HALF), HALF)


TILE_PARTS = ((0, 0, 0), (1, 0, 2), (1, 1, 4))


def lanes_at(i):
    return pl.ds(i * HALF, HALF)


def owner_core(info, which):
    return lax.rem(lax.div(info[which], 3), 2)


def cut_out(info, trailing, earlier, earlier_other, tiles_sent, tiles, columns_sent, columns, share, sems):
    n = trailing.shape[1]
    copies = []

    def copy(a, b):
        copies.append(pltpu.make_async_copy(a, b, sems.at[len(copies)]))
        copies[-1].start()

    for k, (i, j, _) in enumerate(TILE_PARTS):
        rows = pl.ds(tile_start(info, i), B)
        for out, half in ((tiles_sent, 1 - info[4]), (tiles, info[4])):
            copy(trailing.at[rows, half_lanes(tile_start(info, j), half)], out.at[:, lanes_at(k)])
    for j in (0, 1):
        for out, half in ((columns_sent, 1 - info[4]), (columns, info[4])):
            copy(trailing.at[:, half_lanes(tile_start(info, j), half)], out.at[:, lanes_at(j)])
    jobs = []
    for j in (0, 1):
        pairs = [(trailing.at[pl.ds(tile_start(info, j), B), :], share.at[:, pl.ds(j * n, n)])]
        jobs.append((lax.div(info[j], 3) == info[2], pairs, j * n))
    pairs = []
    for t in range(3):
        rows = pl.ds(t * B, B)
        pairs.append((earlier.at[rows, :], share.at[:, pl.ds(2 * n + t * B, HALF)]))
        pairs.append((earlier_other.at[rows, :], share.at[:, pl.ds(2 * n + t * B + HALF, HALF)]))
    jobs.append((info[3] == info[2], pairs, 2 * n))
    at = len(copies)
    for held, pairs, start in jobs:
        sem = [sems.at[at + i] for i in range(len(pairs))]
        at += len(pairs)

        @pl.when(held)
        def _():
            parts = [pltpu.make_async_copy(a, b, s) for (a, b), s in zip(pairs, sem)]
            for c in parts:
                c.start()
            for c in parts:
                c.wait()

        @pl.when(jnp.logical_not(held))
        def _():
            share[:, start : start + n] = jnp.zeros((B, n), BF16)

    for c in copies:
        c.wait()


def keep_tiles(info, tiles, earlier, got, out, sems):
    copies = [
        pltpu.make_async_copy(earlier.at[pl.ds(tile_start(info, i), B), :], out.at[:, lanes_at(2 * i + 1)], sems.at[i])
        for i in (0, 1)
    ]
    for c in copies:
        c.start()
    for k, (_, j, place) in enumerate(TILE_PARTS):
        mine = pltpu.make_async_copy(tiles.at[:, lanes_at(k)], out.at[:, lanes_at(place)], sems.at[2 + k])
        theirs = pltpu.make_async_copy(got.at[:, lanes_at(k)], out.at[:, lanes_at(place)], sems.at[2 + k])
        here = owner_core(info, j) == info[4]
        pl.when(here)(mine.start)
        pl.when(jnp.logical_not(here))(theirs.start)
        copies.append(mine)
    for c in copies:
        c.wait()


def keep_columns(info, columns, got, out, sems):
    copies = []
    for j in (0, 1):
        mine = pltpu.make_async_copy(columns.at[:, lanes_at(j)], out.at[:, lanes_at(j)], sems.at[j])
        theirs = pltpu.make_async_copy(got.at[:, lanes_at(j)], out.at[:, lanes_at(j)], sems.at[j])
        here = owner_core(info, j) == info[4]
        pl.when(here)(mine.start)
        pl.when(jnp.logical_not(here))(theirs.start)
        copies.append(mine)
    for c in copies:
        c.wait()


def copy_call(kernel, shapes, info, args, count, out_spaces):
    return pl.pallas_call(
        kernel,
        out_shape=[jax.ShapeDtypeStruct(shape, BF16) for shape in shapes],
        in_specs=[pl.BlockSpec(memory_space=pltpu.SMEM)] + [pl.BlockSpec(memory_space=pl.ANY)] * len(args),
        out_specs=[pl.BlockSpec(memory_space=space) for space in out_spaces],
        scratch_shapes=[pltpu.SemaphoreType.DMA((count,))],
        compiler_params=pltpu.CompilerParams(vmem_limit_bytes=16 << 20),
        cost_estimate=pl.CostEstimate(flops=10**6, bytes_accessed=1 << 20, transcendentals=0),
        name=kernel.__name__,
    )(info, *args)


barrier = lax.optimization_barrier


def swap(x, axis, mask):
    size = lax.axis_size(axis)
    return lax.ppermute(x, axis, [(i, i ^ mask) for i in range(size)])


def lane_roots(width, parts):
    lane = lax.broadcasted_iota(jnp.int32, (1, width), 1)
    out = jnp.full((1, width), parts[-1][1], jnp.int32)
    for end, root in reversed(parts[:-1]):
        out = jnp.where(lane < end, root, out)
    return out


def ring_sends(chunks, me):
    return tuple(lax.dynamic_index_in_dim(chunks, me ^ k, 0, keepdims=False) for k in (1, 2, 3))


def ring_moves(sent, axis, step):
    return tuple(swap(x, axis, k * step) for x, k in zip(sent, (1, 2, 3)))


def ring_pick(chunks, got, me, root):
    out = lax.dynamic_index_in_dim(chunks, me, 0, keepdims=False)
    for k in (1, 2, 3):
        out = jnp.where((me ^ root) == k, got[k - 1], out)
    return out


def ring_take(chunks, axis, step, me, root):
    return ring_pick(chunks, barrier(ring_moves(barrier(ring_sends(chunks, me)), axis, step)), me, root)


def ring_parts(x, got, me):
    parts = []
    for k in range(4):
        other = me ^ k
        parts.append(
            jnp.where(other == 0, x, jnp.where(other == 1, got[0], jnp.where(other == 2, got[1], got[2])))
        )
    return jnp.concatenate(parts, 0)


def ring_join(x, axis, step, me):
    return ring_parts(x, barrier(ring_moves((x, x, x), axis, step)), me)


def gray(x, bit):
    return ((x >> bit) ^ (x >> (bit + 1))) & 1


def halves(x, bit):
    n = x.shape[0] // 2
    return lax.dynamic_slice_in_dim(x, (1 - bit) * n, n, 0), lax.dynamic_slice_in_dim(x, bit * n, n, 0)


def as_one_step(here, f, *args):
    def nothing(*xs):
        return jax.tree.map(lambda o: jnp.zeros(o.shape, o.dtype), jax.eval_shape(f, *xs))

    return lax.cond(here, f, nothing, *args)


def body(trailing, earlier, block_order):
    z = lax.axis_index("col")
    d = lax.axis_index("depth")
    r = lax.axis_index("row")
    g = 2 * z + d
    n = trailing.shape[0]
    count = n // B
    p0, p1 = block_order[0], block_order[1]
    g0, g1 = p0 // count, p1 // count
    z0, z1 = g0 >> 1, g1 >> 1
    x_here, y_here = r >> 2, r & 3
    info = jnp.stack([p0, p1, r, g, d]).astype(jnp.int32)

    earlier_other = swap(earlier, "depth", 1)
    halves_shape = [(B, 3 * HALF)] * 2 + [(n, B)] * 2
    tiles_sent, tiles, columns_sent, columns, share = copy_call(
        cut_out, halves_shape + [(B, 3 * n)], info, (trailing, earlier, earlier_other), 18, [pl.ANY] * 4 + [pltpu.VMEM]
    )
    got = swap(tiles_sent, "depth", 1)
    columns_got = swap(columns_sent, "depth", 1)
    (pay,) = copy_call(keep_tiles, [(B, 5 * HALF)], info, (tiles, earlier, got), 5, [pl.ANY])
    width = pay.shape[1]
    row_root = lane_roots(width, [(2 * HALF, g0), (width, g1)])
    col_root = lane_roots(width, [(HALF, z0), (2 * HALF, z), (3 * HALF, z0), (4 * HALF, z), (width, z1)])
    chunks = pay.reshape(4, B // 4, width)
    sent, columns, columns_got = barrier((ring_sends(chunks, y_here), columns, columns_got))
    moved = ring_moves(sent, "row", 1)

    (column,) = copy_call(keep_columns, [(n, B)], info, (columns, columns_got), 2, [pl.ANY])
    column_root = lane_roots(B, [(HALF, z0), (B, z1)])
    b1, b2, b3 = gray(z, 0), gray(z, 1), z >> 2
    away, kept = halves(column, b1)

    moved, away, kept, share = barrier((moved, away, kept, share))
    across = lax.psum(share, "row")
    here = p0 >= 0

    def scatter(moved):
        out = ring_pick(chunks, moved, y_here, row_root & 3)
        out = ring_take(out.reshape(4, B // 16, width), "row", 4, x_here, row_root >> 2)
        got = barrier(ring_moves((out,) * 3, "col", 1))
        for k in (1, 2, 3):
            out = jnp.where(((z ^ col_root) & 3) == k, got[k - 1], out)
        return out

    def gather(out):
        out = jnp.where(b3 != col_root >> 2, swap(out, "col", 7), out)
        out = ring_join(out, "row", 4, x_here)
        out = ring_join(out, "row", 1, y_here)
        return out, swap(out, "depth", 1)

    def factors(moved, away, kept):
        got = swap(away, "col", 1)
        state = as_one_step(here, scatter, moved)
        state, got = barrier((state, got))
        away, kept = halves(jnp.where(gray(column_root, 0) != b1, got, kept), b2)
        state, away = barrier((state, away))
        got = swap(away, "col", 3)
        pay, other = as_one_step(here, gather, state)
        pay, other, got = barrier((pay, other, got))
        part = jnp.where(gray(column_root, 1) != b2, got, kept)
        pay, part = barrier((pay, part))
        got = swap(part, "col", 7)
        state = tuple(tile_call(first_factor, [NARROW] * 4 + [WIDE], 2, (pay, other), info))
        state, got = barrier((state, got))
        f0, i0h, i0l, lp1, work = state
        part = jnp.where(b3 != column_root >> 2, got, part)
        work, part = barrier((work, part))
        got = ring_moves((part,) * 3, "col", 1)
        state = tuple(tile_call(second_factor, [NARROW] * 3, 2, (work,)))
        state, got = barrier((state, got))
        f1, i1h, i1l = state
        whole = ring_parts(part, (got[2], got[0], got[1]), 2 * b1 + b2)
        return whole, swap(whole, "depth", 1), pay, other, f0, i0h, i0l, lp1, f1, i1h, i1l

    column, column_other, *rest = as_one_step(here, factors, moved, away, kept)
    panels, out = update(
        info,
        [trailing, column, column_other, earlier, earlier_other],
        [across, *rest],
    )
    return panels, out


def solution(mesh):
    placed = (P("row", ("col", "depth")), P("row", "depth"), P())
    return jax.shard_map(
        body,
        mesh=mesh,
        in_specs=placed,
        out_specs=(P("row", "depth"), P("row", ("col", "depth"))),
        check_vma=False,
    )
```

```python
import jax
import jax.numpy as jnp
from jax import lax
from jax.experimental import pallas as pl
from jax.experimental.pallas import tpu as pltpu
from jax.sharding import PartitionSpec as P

B = 512
F32 = jnp.float32
BF16 = jnp.bfloat16
HIGHEST = lax.Precision.HIGHEST


def pivot_block(d):
    n = 8
    d = [row[:] for row in d]
    low = [[None] * n for _ in range(n)]
    inv = [None] * n
    diag = [None] * n
    for j in range(0, n, 2):
        a, b, c = d[j][j], d[j + 1][j], d[j + 1][j + 1]
        det = a * c - b * b
        inv[j] = 1.0 / a
        inv_det = 1.0 / det
        inv[j + 1] = a * inv_det
        diag[j] = a
        diag[j + 1] = det * inv[j]
        low[j + 1][j] = b * inv[j]
        for i in range(j + 2, n):
            low[i][j] = d[i][j] * inv[j]
            low[i][j + 1] = (a * d[i][j + 1] - b * d[i][j]) * inv_det
        for i in range(j + 2, n):
            first = (c * d[i][j] - b * d[i][j + 1]) * inv_det
            for k in range(j + 2, i + 1):
                d[i][k] = d[i][k] - (first * d[k][j] + low[i][j + 1] * d[k][j + 1])
    return low, inv, diag


def chol_128(work, upper, base):
    lane = lax.broadcasted_iota(jnp.int32, (8, 128), 1)
    blocks = [work[base + 8 * m : base + 8 * m + 8, base : base + 128] for m in range(16)]

    def over_lanes(x, k):
        return jnp.broadcast_to(x[:, k : k + 1], (8, 128))

    def over_rows(x, k):
        return jnp.broadcast_to(x[k : k + 1, :], (8, 128))

    for q in range(16):
        o = 8 * q
        pivot = blocks[q]
        cols = [over_lanes(pivot, o + j) for j in range(8)]
        entries = [[over_rows(cols[j], i) if j <= i else None for j in range(8)] for i in range(8)]
        low, inv, diag = pivot_block(entries)
        inside = (lane >= o) & (lane < o + 8)
        solved = []
        for j in range(8):
            u = jnp.where(inside, jnp.where(lane == o + j, 1.0, 0.0), over_rows(pivot, j))
            for i in range(j):
                u = u - low[j][i] * solved[i]
            solved.append(u)
        if q < 15:
            back = [None] * 8
            for i in reversed(range(8)):
                g = solved[i] * inv[i]
                for j in range(i + 1, 8):
                    g = g - low[j][i] * back[j]
                back[i] = g
            for m in range(q + 1, 16):
                x = blocks[m]
                acc = jnp.where(inside, 0.0, x)
                for i in range(8):
                    acc = acc - over_lanes(x, o + i) * back[i]
                blocks[m] = acc
        for j in range(8):
            scale = lax.rsqrt(diag[j])
            root = diag[j] * scale
            row = solved[j] * scale
            up = jnp.where(lane < o + 8, 0.0, row)
            up = jnp.where(lane == o + j, root, up)
            for i in range(j + 1, 8):
                up = jnp.where(lane == o + i, low[i][j] * root, up)
            upper[base + o + j : base + o + j + 1, base : base + 128] = up[0:1]
            work[base + o + j : base + o + j + 1, base : base + 128] = jnp.where(lane <= o + j, row, 0.0)[0:1]


def dot(a, b, ca, cb, precision=None):
    return lax.dot_general(a, b, (((ca,), (cb,)), ((), ())), precision=precision, preferred_element_type=F32)


def chol_strips(work, upper, strips):
    for b in strips:
        o = 128 * b
        e = o + 128
        chol_128(work, upper, o)
        inv = work[o:e, o:e]
        if b > 0:
            work[o:e, 0:o] = dot(inv, work[o:e, 0:o], 1, 0, HIGHEST)
            upper[o:e, 0:o] = jnp.zeros((128, o), F32)
        if b < 3:
            up = dot(inv, work[o:e, e:B], 1, 0, HIGHEST)
            upper[o:e, e:B] = up
            work[o:e, e:B] = jnp.zeros_like(up)
            work[e:B, o:e] = jnp.zeros((B - e, 128), F32)
            work[e:B, 0:e] = work[e:B, 0:e] - dot(up, work[o:e, 0:e], 0, 0, HIGHEST)
            work[e:B, e:B] = work[e:B, e:B] - dot(up, up, 0, 0, HIGHEST)


def split(x):
    hi = x.astype(BF16)
    return hi, (x - hi.astype(F32)).astype(BF16)


def dot3(a, b, ca, cb):
    return dot(a[0], b[0], ca, cb) + (dot(a[0], b[1], ca, cb) + dot(a[1], b[0], ca, cb))


def times_lower_t(x, low):
    h = B // 2
    left = dot3([v[:, :h] for v in x], [v[:h, :h] for v in low], 1, 1)
    return jnp.concatenate([left, dot3(x, [v[h:] for v in low], 1, 1)], 1)


def lower_times(low, x):
    h = B // 2
    top = dot3([v[:h, :h] for v in low], [v[:h] for v in x], 1, 0)
    return jnp.concatenate([top, dot3([v[h:] for v in low], x, 1, 0)], 0)


def symmetric(x):
    return 0.5 * (x + x.T)


def by_core(info, own, other):
    first = info[4] == 0
    own, other = own.astype(F32), other.astype(F32)
    return jnp.concatenate([jnp.where(first, own, other), jnp.where(first, other, own)], 1)


HALF = B // 2


def payload_part(own, other, index):
    lanes = slice(index * HALF, index * HALF + HALF)
    return own[:, lanes], other[:, lanes]


def payload_tile(info, own, other, index):
    return by_core(info, *payload_part(own, other, index))


def payload_rows(own, other, index):
    return jnp.concatenate(payload_part(own, other, index), 1)


def finish(work, upper, f, ih, il):
    f[...] = upper[...].T.astype(BF16)
    h, l = split(work[...])
    ih[...] = h
    il[...] = l


def first_factor(info, own, other, f, ih, il, lp, next_work, work, upper):
    ep0 = payload_rows(own, other, 1)
    ep1 = payload_rows(own, other, 3)
    work[...] = symmetric(payload_tile(info, own, other, 0) - dot(ep0, ep0, 1, 1))
    chol_strips(work, upper, (0, 1, 2, 3))
    finish(work, upper, f, ih, il)
    c10 = payload_tile(info, own, other, 2) - dot(ep1, ep0, 1, 1)
    lp[...] = dot3(split(c10), (ih[...], il[...]), 1, 1).astype(BF16)
    c11 = payload_tile(info, own, other, 4) - dot(ep1, ep1, 1, 1) - dot(lp[...], lp[...], 1, 1)
    next_work[...] = symmetric(c11)


def second_factor(work_in, f, ih, il, work, upper):
    work[...] = work_in[...]
    chol_strips(work, upper, (0, 1, 2, 3))
    finish(work, upper, f, ih, il)


WIDE = jax.ShapeDtypeStruct((B, B), F32)
NARROW = jax.ShapeDtypeStruct((B, B), BF16)


def tile_call(kernel, out_shape, scratch, args, info=None):
    def spec(_):
        return pl.BlockSpec(memory_space=pltpu.VMEM)

    specs = [spec(a) for a in args]
    if info is not None:
        specs = [pl.BlockSpec(memory_space=pltpu.SMEM)] + specs
        args = [info] + list(args)
    return pl.pallas_call(
        kernel,
        out_shape=out_shape,
        in_specs=specs,
        out_specs=[spec(a) for a in out_shape],
        scratch_shapes=[pltpu.VMEM((B, B), F32)] * scratch,
        compiler_params=pltpu.CompilerParams(vmem_limit_bytes=32 << 20),
        cost_estimate=pl.CostEstimate(flops=10**6, bytes_accessed=1 << 20, transcendentals=0),
        name=kernel.__name__,
    )(*args)


def columns_kernel(r0, r1, eg, pay_own, pay_oth, i0h, i0l, lp1, i1h, i1l, l0t, l1t):
    ep0 = payload_rows(pay_own, pay_oth, 1)
    ep1 = payload_rows(pay_own, pay_oth, 3)
    c0 = r0[...].astype(F32) - dot(ep0, eg[...], 1, 1)
    l0 = lower_times((i0h[...], i0l[...]), split(c0)).astype(BF16)
    l0t[...] = l0
    c1 = r1[...].astype(F32) - dot(ep1, eg[...], 1, 1) - dot(lp1[...], l0, 1, 0)
    l1t[...] = lower_times((i1h[...], i1l[...]), split(c1)).astype(BF16)


def columns_of(across, *whole):
    count = across.shape[1] // B // 3

    def lanes(first):
        return pl.BlockSpec((B, B), lambda t: (0, first + t))

    return pl.pallas_call(
        columns_kernel,
        out_shape=[jax.ShapeDtypeStruct((B, count * B), BF16)] * 2,
        grid=(count,),
        in_specs=[lanes(0), lanes(count), lanes(2 * count)] + [pl.BlockSpec(x.shape, lambda t: (0, 0)) for x in whole],
        out_specs=[lanes(0)] * 2,
        compiler_params=pltpu.CompilerParams(vmem_limit_bytes=56 << 20),
        cost_estimate=pl.CostEstimate(flops=6 * 10**9, bytes_accessed=12 << 20, transcendentals=0),
        name="columns",
    )(across, across, across, *whole)


def update_kernel(
    info, trailing, col_own, col_oth, er_own, er_oth, across, l0t, l1t, pay_own, pay_oth,
    f0, i0h, i0l, lp1, f1, i1h, i1l, panels, out,
):
    step = pl.program_id(0)
    p0, p1 = info[0], info[1]
    i0 = (i0h[...], i0l[...])
    i1 = (i1h[...], i1l[...])
    ep0 = payload_rows(pay_own, pay_oth, 1)
    ep1 = payload_rows(pay_own, pay_oth, 3)

    tile = info[2] * 3 + step
    er = jnp.concatenate([er_own[...], er_oth[...]], 1)
    c0 = by_core(info, col_own[:, :HALF], col_oth[:, :HALF]) - dot(er, ep0, 1, 1)
    l0 = times_lower_t(split(c0), i0).astype(BF16)
    l0 = jnp.where(tile == p0, f0[...], l0)
    c1 = by_core(info, col_own[:, HALF:], col_oth[:, HALF:]) - dot(er, ep1, 1, 1) - dot(l0, lp1[...], 1, 1)
    l1 = times_lower_t(split(c1), i1).astype(BF16)
    l1 = jnp.where(tile == p1, f1[...], l1)
    l1 = jnp.where(tile == p0, jnp.zeros_like(l1), l1)
    panels[...] = jnp.where(info[4] == 0, l0, l1)
    row_kept = jnp.logical_and(tile != p0, tile != p1)
    for t in range(3):
        cols = slice(t * B, t * B + B)
        col_tile = info[3] * 3 + t
        kept = jnp.logical_and(row_kept, jnp.logical_and(col_tile != p0, col_tile != p1))
        c = trailing[:, cols].astype(F32) - (
            dot(er, across[:, cols], 1, 1) + dot(l0, l0t[:, cols], 1, 0) + dot(l1, l1t[:, cols], 1, 0)
        )
        out[:, cols] = jnp.where(kept, c, 0.0).astype(BF16)


def update(info, by_rows, across, whole):
    n = by_rows[0].shape[0]

    def rows(x):
        return pl.BlockSpec((B, x.shape[1]), lambda i, s: (i, 0))

    def all_of(x):
        return pl.BlockSpec(x.shape, lambda i, s: (0, 0))

    out_shape = [jax.ShapeDtypeStruct((n, B), BF16), jax.ShapeDtypeStruct((n, n), BF16)]
    return pl.pallas_call(
        update_kernel,
        out_shape=out_shape,
        grid_spec=pltpu.PrefetchScalarGridSpec(
            num_scalar_prefetch=1,
            grid=(n // B,),
            in_specs=[rows(x) for x in by_rows]
            + [pl.BlockSpec((B, n), lambda i, s: (0, 2))]
            + [all_of(x) for x in whole],
            out_specs=[rows(x) for x in out_shape],
        ),
        compiler_params=pltpu.CompilerParams(vmem_limit_bytes=56 << 20),
        cost_estimate=pl.CostEstimate(flops=25 * 10**9, bytes_accessed=24 << 20, transcendentals=0),
        name="update",
    )(info, *by_rows, across, *whole)


def tile_start(info, which):
    return pl.multiple_of(lax.rem(info[which], 3) * B, B)


def half_lanes(start, half):
    return pl.ds(pl.multiple_of(start + half * HALF, HALF), HALF)


TILE_PARTS = ((0, 0, 0), (1, 0, 2), (1, 1, 4))


def lanes_at(i):
    return pl.ds(i * HALF, HALF)


def owner_core(info, which):
    return lax.rem(lax.div(info[which], 3), 2)


def cut_out(info, trailing, tiles_sent, tiles, columns_sent, columns, sems):
    copies = []

    def copy(a, b):
        copies.append(pltpu.make_async_copy(a, b, sems.at[len(copies)]))
        copies[-1].start()

    for k, (i, j, _) in enumerate(TILE_PARTS):
        rows = pl.ds(tile_start(info, i), B)
        for out, half in ((tiles_sent, 1 - info[4]), (tiles, info[4])):
            copy(trailing.at[rows, half_lanes(tile_start(info, j), half)], out.at[:, lanes_at(k)])
    for j in (0, 1):
        for out, half in ((columns_sent, 1 - info[4]), (columns, info[4])):
            copy(trailing.at[:, half_lanes(tile_start(info, j), half)], out.at[:, lanes_at(j)])
    for c in copies:
        c.wait()


def rows_to_sum(info, trailing, earlier, earlier_other, share, sems):
    n = trailing.shape[1]
    jobs = []
    for j in (0, 1):
        pairs = [(trailing.at[pl.ds(tile_start(info, j), B), :], share.at[:, pl.ds(j * n, n)])]
        jobs.append((lax.div(info[j], 3) == info[2], pairs, j * n))
    pairs = []
    for t in range(3):
        rows = pl.ds(t * B, B)
        pairs.append((earlier.at[rows, :], share.at[:, pl.ds(2 * n + t * B, HALF)]))
        pairs.append((earlier_other.at[rows, :], share.at[:, pl.ds(2 * n + t * B + HALF, HALF)]))
    jobs.append((info[3] == info[2], pairs, 2 * n))
    at = 0
    for held, pairs, start in jobs:
        sem = [sems.at[at + i] for i in range(len(pairs))]
        at += len(pairs)

        @pl.when(held)
        def _():
            parts = [pltpu.make_async_copy(a, b, s) for (a, b), s in zip(pairs, sem)]
            for c in parts:
                c.start()
            for c in parts:
                c.wait()

        @pl.when(jnp.logical_not(held))
        def _():
            share[:, start : start + n] = jnp.zeros((B, n), BF16)


def keep_tiles(info, tiles, earlier, got, out, sems):
    copies = [
        pltpu.make_async_copy(earlier.at[pl.ds(tile_start(info, i), B), :], out.at[:, lanes_at(2 * i + 1)], sems.at[i])
        for i in (0, 1)
    ]
    for c in copies:
        c.start()
    for k, (_, j, place) in enumerate(TILE_PARTS):
        mine = pltpu.make_async_copy(tiles.at[:, lanes_at(k)], out.at[:, lanes_at(place)], sems.at[2 + k])
        theirs = pltpu.make_async_copy(got.at[:, lanes_at(k)], out.at[:, lanes_at(place)], sems.at[2 + k])
        here = owner_core(info, j) == info[4]
        pl.when(here)(mine.start)
        pl.when(jnp.logical_not(here))(theirs.start)
        copies.append(mine)
    for c in copies:
        c.wait()


def keep_columns(info, columns, got, out, sems):
    copies = []
    for j in (0, 1):
        mine = pltpu.make_async_copy(columns.at[:, lanes_at(j)], out.at[:, lanes_at(j)], sems.at[j])
        theirs = pltpu.make_async_copy(got.at[:, lanes_at(j)], out.at[:, lanes_at(j)], sems.at[j])
        here = owner_core(info, j) == info[4]
        pl.when(here)(mine.start)
        pl.when(jnp.logical_not(here))(theirs.start)
        copies.append(mine)
    for c in copies:
        c.wait()


def copy_call(kernel, shapes, info, args, count, out_spaces):
    return pl.pallas_call(
        kernel,
        out_shape=[jax.ShapeDtypeStruct(shape, BF16) for shape in shapes],
        in_specs=[pl.BlockSpec(memory_space=pltpu.SMEM)] + [pl.BlockSpec(memory_space=pl.ANY)] * len(args),
        out_specs=[pl.BlockSpec(memory_space=space) for space in out_spaces],
        scratch_shapes=[pltpu.SemaphoreType.DMA((count,))],
        compiler_params=pltpu.CompilerParams(vmem_limit_bytes=16 << 20),
        cost_estimate=pl.CostEstimate(flops=10**6, bytes_accessed=1 << 20, transcendentals=0),
        name=kernel.__name__,
    )(info, *args)


barrier = lax.optimization_barrier


def swap(x, axis, mask):
    size = lax.axis_size(axis)
    return lax.ppermute(x, axis, [(i, i ^ mask) for i in range(size)])


def lane_roots(width, parts):
    lane = lax.broadcasted_iota(jnp.int32, (1, width), 1)
    out = jnp.full((1, width), parts[-1][1], jnp.int32)
    for end, root in reversed(parts[:-1]):
        out = jnp.where(lane < end, root, out)
    return out


def ring_sends(chunks, me):
    return tuple(lax.dynamic_index_in_dim(chunks, me ^ k, 0, keepdims=False) for k in (1, 2, 3))


def ring_moves(sent, axis, step):
    return tuple(swap(x, axis, k * step) for x, k in zip(sent, (1, 2, 3)))


def ring_pick(chunks, got, me, root):
    out = lax.dynamic_index_in_dim(chunks, me, 0, keepdims=False)
    for k in (1, 2, 3):
        out = jnp.where((me ^ root) == k, got[k - 1], out)
    return out


def ring_take(chunks, axis, step, me, root):
    return ring_pick(chunks, barrier(ring_moves(barrier(ring_sends(chunks, me)), axis, step)), me, root)


def ring_parts(x, got, me):
    parts = []
    for k in range(4):
        other = me ^ k
        parts.append(
            jnp.where(other == 0, x, jnp.where(other == 1, got[0], jnp.where(other == 2, got[1], got[2])))
        )
    return jnp.concatenate(parts, 0)


def ring_join(x, axis, step, me):
    return ring_parts(x, barrier(ring_moves((x, x, x), axis, step)), me)


def gray(x, bit):
    return ((x >> bit) ^ (x >> (bit + 1))) & 1


def halves(x, bit):
    n = x.shape[0] // 2
    return lax.dynamic_slice_in_dim(x, (1 - bit) * n, n, 0), lax.dynamic_slice_in_dim(x, bit * n, n, 0)


def as_one_step(here, f, *args):
    def nothing(*xs):
        return jax.tree.map(lambda o: jnp.zeros(o.shape, o.dtype), jax.eval_shape(f, *xs))

    return lax.cond(here, f, nothing, *args)


def body(trailing, earlier, block_order):
    z = lax.axis_index("col")
    d = lax.axis_index("depth")
    r = lax.axis_index("row")
    g = 2 * z + d
    n = trailing.shape[0]
    count = n // B
    p0, p1 = block_order[0], block_order[1]
    g0, g1 = p0 // count, p1 // count
    z0, z1 = g0 >> 1, g1 >> 1
    x_here, y_here = r >> 2, r & 3
    info = jnp.stack([p0, p1, r, g, d]).astype(jnp.int32)

    earlier_other = swap(earlier, "depth", 1)
    shapes = [(B, 3 * HALF)] * 2 + [(n, B)] * 2
    tiles_sent, tiles, columns_sent, columns = copy_call(cut_out, shapes, info, (trailing,), 10, [pl.ANY] * 4)
    got, columns_sent = barrier((swap(tiles_sent, "depth", 1), columns_sent))
    columns_got = swap(columns_sent, "depth", 1)
    (pay,) = copy_call(keep_tiles, [(B, 5 * HALF)], info, (tiles, earlier, got), 5, [pl.ANY])
    width = pay.shape[1]
    row_root = lane_roots(width, [(2 * HALF, g0), (width, g1)])
    col_root = lane_roots(width, [(HALF, z0), (2 * HALF, z), (3 * HALF, z0), (4 * HALF, z), (width, z1)])
    chunks = pay.reshape(4, B // 4, width)
    sent, info_b = barrier((ring_sends(chunks, y_here), info))
    moved = ring_moves(sent, "row", 1)

    (column,) = copy_call(keep_columns, [(n, B)], info_b, (columns, columns_got), 2, [pl.ANY])
    column_root = lane_roots(B, [(HALF, z0), (B, z1)])
    b1, b2, b3 = gray(z, 0), gray(z, 1), z >> 2
    away, kept = halves(column, b1)

    (share,) = copy_call(
        rows_to_sum, [(B, 3 * n)], info_b, (trailing, earlier, earlier_other), 8, [pltpu.VMEM]
    )
    moved, away, kept, share = barrier((moved, away, kept, share))
    across = lax.psum(share, "row")
    here = p0 >= 0

    def scatter(moved):
        out = ring_pick(chunks, moved, y_here, row_root & 3)
        out = ring_take(out.reshape(4, B // 16, width), "row", 4, x_here, row_root >> 2)
        got = barrier(ring_moves((out,) * 3, "col", 1))
        for k in (1, 2, 3):
            out = jnp.where(((z ^ col_root) & 3) == k, got[k - 1], out)
        return out

    def gather(out):
        out = jnp.where(b3 != col_root >> 2, swap(out, "col", 7), out)
        out = ring_join(out, "row", 4, x_here)
        out = ring_join(out, "row", 1, y_here)
        return out, swap(out, "depth", 1)

    def factors(moved, away, kept):
        got = swap(away, "col", 1)
        state = as_one_step(here, scatter, moved)
        state, got = barrier((state, got))
        away, kept = halves(jnp.where(gray(column_root, 0) != b1, got, kept), b2)
        state, away = barrier((state, away))
        got = swap(away, "col", 3)
        pay, other = as_one_step(here, gather, state)
        pay, other, got = barrier((pay, other, got))
        part = jnp.where(gray(column_root, 1) != b2, got, kept)
        pay, part = barrier((pay, part))
        got = swap(part, "col", 7)
        state = tuple(tile_call(first_factor, [NARROW] * 4 + [WIDE], 2, (pay, other), info))
        state, got = barrier((state, got))
        f0, i0h, i0l, lp1, work = state
        part = jnp.where(b3 != column_root >> 2, got, part)
        work, part = barrier((work, part))
        got = ring_moves((part,) * 3, "col", 1)
        state = tuple(tile_call(second_factor, [NARROW] * 3, 2, (work,)))
        state, got = barrier((state, got))
        f1, i1h, i1l = state
        whole = ring_parts(part, (got[2], got[0], got[1]), 2 * b1 + b2)
        return whole, pay, other, f0, i0h, i0l, lp1, f1, i1h, i1l

    column, pay, other, f0, i0h, i0l, lp1, f1, i1h, i1l = as_one_step(here, factors, moved, away, kept)
    column_other = swap(column, "depth", 1)
    l0t, l1t = columns_of(across, pay, other, i0h, i0l, lp1, i1h, i1l)
    panels, out = update(
        info,
        [trailing, column, column_other, earlier, earlier_other],
        across,
        [l0t, l1t, pay, other, f0, i0h, i0l, lp1, f1, i1h, i1l],
    )
    return panels, out


def solution(mesh):
    placed = (P("row", ("col", "depth")), P("row", "depth"), P())
    return jax.shard_map(
        body,
        mesh=mesh,
        in_specs=placed,
        out_specs=(P("row", "depth"), P("row", ("col", "depth"))),
        check_vma=False,
    )
```

```python
import jax
import jax.numpy as jnp
from jax import lax
from jax.experimental import pallas as pl
from jax.experimental.pallas import tpu as pltpu
from jax.sharding import PartitionSpec as P

B = 512
F32 = jnp.float32
BF16 = jnp.bfloat16
HIGHEST = lax.Precision.HIGHEST


def pivot_block(d):
    n = 8
    d = [row[:] for row in d]
    low = [[None] * n for _ in range(n)]
    inv = [None] * n
    diag = [None] * n
    for j in range(0, n, 2):
        a, b, c = d[j][j], d[j + 1][j], d[j + 1][j + 1]
        det = a * c - b * b
        inv[j] = 1.0 / a
        inv_det = 1.0 / det
        inv[j + 1] = a * inv_det
        diag[j] = a
        diag[j + 1] = det * inv[j]
        low[j + 1][j] = b * inv[j]
        for i in range(j + 2, n):
            low[i][j] = d[i][j] * inv[j]
            low[i][j + 1] = (a * d[i][j + 1] - b * d[i][j]) * inv_det
        for i in range(j + 2, n):
            first = (c * d[i][j] - b * d[i][j + 1]) * inv_det
            for k in range(j + 2, i + 1):
                d[i][k] = d[i][k] - (first * d[k][j] + low[i][j + 1] * d[k][j + 1])
    return low, inv, diag


def chol_128(work, upper, base):
    lane = lax.broadcasted_iota(jnp.int32, (8, 128), 1)
    blocks = [work[base + 8 * m : base + 8 * m + 8, base : base + 128] for m in range(16)]

    def over_lanes(x, k):
        return jnp.broadcast_to(x[:, k : k + 1], (8, 128))

    def over_rows(x, k):
        return jnp.broadcast_to(x[k : k + 1, :], (8, 128))

    for q in range(16):
        o = 8 * q
        pivot = blocks[q]
        cols = [over_lanes(pivot, o + j) for j in range(8)]
        entries = [[over_rows(cols[j], i) if j <= i else None for j in range(8)] for i in range(8)]
        low, inv, diag = pivot_block(entries)
        inside = (lane >= o) & (lane < o + 8)
        solved = []
        for j in range(8):
            u = jnp.where(inside, jnp.where(lane == o + j, 1.0, 0.0), over_rows(pivot, j))
            for i in range(j):
                u = u - low[j][i] * solved[i]
            solved.append(u)
        if q < 15:
            back = [None] * 8
            for i in reversed(range(8)):
                g = solved[i] * inv[i]
                for j in range(i + 1, 8):
                    g = g - low[j][i] * back[j]
                back[i] = g
            for m in range(q + 1, 16):
                x = blocks[m]
                acc = jnp.where(inside, 0.0, x)
                for i in range(8):
                    acc = acc - over_lanes(x, o + i) * back[i]
                blocks[m] = acc
        for j in range(8):
            scale = lax.rsqrt(diag[j])
            root = diag[j] * scale
            row = solved[j] * scale
            up = jnp.where(lane < o + 8, 0.0, row)
            up = jnp.where(lane == o + j, root, up)
            for i in range(j + 1, 8):
                up = jnp.where(lane == o + i, low[i][j] * root, up)
            upper[base + o + j : base + o + j + 1, base : base + 128] = up[0:1]
            work[base + o + j : base + o + j + 1, base : base + 128] = jnp.where(lane <= o + j, row, 0.0)[0:1]


def dot(a, b, ca, cb, precision=None):
    return lax.dot_general(a, b, (((ca,), (cb,)), ((), ())), precision=precision, preferred_element_type=F32)


def chol_strips(work, upper, strips):
    for b in strips:
        o = 128 * b
        e = o + 128
        chol_128(work, upper, o)
        inv = work[o:e, o:e]
        if b > 0:
            work[o:e, 0:o] = dot(inv, work[o:e, 0:o], 1, 0, HIGHEST)
            upper[o:e, 0:o] = jnp.zeros((128, o), F32)
        if b < 3:
            up = dot(inv, work[o:e, e:B], 1, 0, HIGHEST)
            upper[o:e, e:B] = up
            work[o:e, e:B] = jnp.zeros_like(up)
            work[e:B, o:e] = jnp.zeros((B - e, 128), F32)
            work[e:B, 0:e] = work[e:B, 0:e] - dot(up, work[o:e, 0:e], 0, 0, HIGHEST)
            work[e:B, e:B] = work[e:B, e:B] - dot(up, up, 0, 0, HIGHEST)


def split(x):
    hi = x.astype(BF16)
    return hi, (x - hi.astype(F32)).astype(BF16)


def dot3(a, b, ca, cb):
    return dot(a[0], b[0], ca, cb) + (dot(a[0], b[1], ca, cb) + dot(a[1], b[0], ca, cb))


def times_lower_t(x, low):
    h = B // 2
    left = dot3([v[:, :h] for v in x], [v[:h, :h] for v in low], 1, 1)
    return jnp.concatenate([left, dot3(x, [v[h:] for v in low], 1, 1)], 1)


def lower_times(low, x):
    h = B // 2
    top = dot3([v[:h, :h] for v in low], [v[:h] for v in x], 1, 0)
    return jnp.concatenate([top, dot3([v[h:] for v in low], x, 1, 0)], 0)


def symmetric(x):
    return 0.5 * (x + x.T)


def by_core(info, own, other):
    first = info[4] == 0
    own, other = own.astype(F32), other.astype(F32)
    return jnp.concatenate([jnp.where(first, own, other), jnp.where(first, other, own)], 1)


HALF = B // 2


def payload_part(own, other, index):
    lanes = slice(index * HALF, index * HALF + HALF)
    return own[:, lanes], other[:, lanes]


def payload_tile(info, own, other, index):
    return by_core(info, *payload_part(own, other, index))


def payload_rows(own, other, index):
    return jnp.concatenate(payload_part(own, other, index), 1)


def finish(work, upper, f, ih, il):
    f[...] = upper[...].T.astype(BF16)
    h, l = split(work[...])
    ih[...] = h
    il[...] = l


def first_factor(info, own, other, f, ih, il, lp, next_work, work, upper):
    ep0 = payload_rows(own, other, 1)
    ep1 = payload_rows(own, other, 3)
    work[...] = symmetric(payload_tile(info, own, other, 0) - dot(ep0, ep0, 1, 1))
    chol_strips(work, upper, (0, 1, 2, 3))
    finish(work, upper, f, ih, il)
    c10 = payload_tile(info, own, other, 2) - dot(ep1, ep0, 1, 1)
    lp[...] = dot3(split(c10), (ih[...], il[...]), 1, 1).astype(BF16)
    c11 = payload_tile(info, own, other, 4) - dot(ep1, ep1, 1, 1) - dot(lp[...], lp[...], 1, 1)
    next_work[...] = symmetric(c11)


def second_factor(work_in, f, ih, il, work, upper):
    work[...] = work_in[...]
    chol_strips(work, upper, (0, 1, 2, 3))
    finish(work, upper, f, ih, il)


WIDE = jax.ShapeDtypeStruct((B, B), F32)
NARROW = jax.ShapeDtypeStruct((B, B), BF16)


def tile_call(kernel, out_shape, scratch, args, info=None):
    def spec(_):
        return pl.BlockSpec(memory_space=pltpu.VMEM)

    specs = [spec(a) for a in args]
    if info is not None:
        specs = [pl.BlockSpec(memory_space=pltpu.SMEM)] + specs
        args = [info] + list(args)
    return pl.pallas_call(
        kernel,
        out_shape=out_shape,
        in_specs=specs,
        out_specs=[spec(a) for a in out_shape],
        scratch_shapes=[pltpu.VMEM((B, B), F32)] * scratch,
        compiler_params=pltpu.CompilerParams(vmem_limit_bytes=32 << 20),
        cost_estimate=pl.CostEstimate(flops=10**6, bytes_accessed=1 << 20, transcendentals=0),
        name=kernel.__name__,
    )(*args)


def columns_kernel(r0, r1, eg, ep0_own, ep0_oth, ep1_own, ep1_oth, i0h, i0l, lp1, i1h, i1l, l0t, l1t):
    ep0 = jnp.concatenate([ep0_own[...], ep0_oth[...]], 1)
    ep1 = jnp.concatenate([ep1_own[...], ep1_oth[...]], 1)
    c0 = r0[...].astype(F32) - dot(ep0, eg[...], 1, 1)
    l0 = lower_times((i0h[...], i0l[...]), split(c0)).astype(BF16)
    l0t[...] = l0
    c1 = r1[...].astype(F32) - dot(ep1, eg[...], 1, 1) - dot(lp1[...], l0, 1, 0)
    l1t[...] = lower_times((i1h[...], i1l[...]), split(c1)).astype(BF16)


def fixed(shape, lane_block):
    return pl.BlockSpec(shape, lambda *_: (0, lane_block), pipeline_mode=pl.Buffered(1))


def earlier_specs():
    return [fixed((B, HALF), 1), fixed((B, HALF), 1), fixed((B, HALF), 3), fixed((B, HALF), 3)]


def columns_of(across, pay, other, *whole):
    count = across.shape[1] // B // 3

    def lanes(first):
        return pl.BlockSpec((B, B), lambda t: (0, first + t))

    return pl.pallas_call(
        columns_kernel,
        out_shape=[jax.ShapeDtypeStruct((B, count * B), BF16)] * 2,
        grid=(count,),
        in_specs=[lanes(0), lanes(count), lanes(2 * count)]
        + earlier_specs()
        + [fixed(x.shape, 0) for x in whole],
        out_specs=[lanes(0)] * 2,
        compiler_params=pltpu.CompilerParams(vmem_limit_bytes=56 << 20),
        cost_estimate=pl.CostEstimate(flops=6 * 10**9, bytes_accessed=12 << 20, transcendentals=0),
        name="columns",
    )(across, across, across, pay, other, pay, other, *whole)


def update_kernel(
    info, trailing, col_own, col_oth, er_own, er_oth, across, l0t, l1t, ep0_own, ep0_oth, ep1_own, ep1_oth,
    f0, i0h, i0l, lp1, f1, i1h, i1l, panels, out,
):
    step = pl.program_id(0)
    p0, p1 = info[0], info[1]
    i0 = (i0h[...], i0l[...])
    i1 = (i1h[...], i1l[...])
    ep0 = jnp.concatenate([ep0_own[...], ep0_oth[...]], 1)
    ep1 = jnp.concatenate([ep1_own[...], ep1_oth[...]], 1)

    tile = info[2] * 3 + step
    er = jnp.concatenate([er_own[...], er_oth[...]], 1)
    c0 = by_core(info, col_own[:, :HALF], col_oth[:, :HALF]) - dot(er, ep0, 1, 1)
    l0 = times_lower_t(split(c0), i0).astype(BF16)
    l0 = jnp.where(tile == p0, f0[...], l0)
    c1 = by_core(info, col_own[:, HALF:], col_oth[:, HALF:]) - dot(er, ep1, 1, 1) - dot(l0, lp1[...], 1, 1)
    l1 = times_lower_t(split(c1), i1).astype(BF16)
    l1 = jnp.where(tile == p1, f1[...], l1)
    l1 = jnp.where(tile == p0, jnp.zeros_like(l1), l1)
    panels[...] = jnp.where(info[4] == 0, l0, l1)
    row_kept = jnp.logical_and(tile != p0, tile != p1)
    for t in range(3):
        cols = slice(t * B, t * B + B)
        col_tile = info[3] * 3 + t
        kept = jnp.logical_and(row_kept, jnp.logical_and(col_tile != p0, col_tile != p1))
        c = trailing[:, cols].astype(F32) - (
            dot(er, across[:, cols], 1, 1) + dot(l0, l0t[:, cols], 1, 0) + dot(l1, l1t[:, cols], 1, 0)
        )
        out[:, cols] = jnp.where(kept, c, 0.0).astype(BF16)


def update(info, by_rows, across, turned, pay, other, whole):
    n = by_rows[0].shape[0]

    def rows(x):
        return pl.BlockSpec((B, x.shape[1]), lambda i, s: (i, 0))

    out_shape = [jax.ShapeDtypeStruct((n, B), BF16), jax.ShapeDtypeStruct((n, n), BF16)]
    return pl.pallas_call(
        update_kernel,
        out_shape=out_shape,
        grid_spec=pltpu.PrefetchScalarGridSpec(
            num_scalar_prefetch=1,
            grid=(n // B,),
            in_specs=[rows(x) for x in by_rows]
            + [fixed((B, n), 2)]
            + [fixed(x.shape, 0) for x in turned]
            + earlier_specs()
            + [fixed(x.shape, 0) for x in whole],
            out_specs=[rows(x) for x in out_shape],
        ),
        compiler_params=pltpu.CompilerParams(vmem_limit_bytes=40 << 20),
        cost_estimate=pl.CostEstimate(flops=25 * 10**9, bytes_accessed=24 << 20, transcendentals=0),
        name="update",
    )(info, *by_rows, across, *turned, pay, other, pay, other, *whole)


def tile_start(info, which):
    return pl.multiple_of(lax.rem(info[which], 3) * B, B)


def half_lanes(start, half):
    return pl.ds(pl.multiple_of(start + half * HALF, HALF), HALF)


TILE_PARTS = ((0, 0, 0), (1, 0, 2), (1, 1, 4))


def lanes_at(i):
    return pl.ds(i * HALF, HALF)


def owner_core(info, which):
    return lax.rem(lax.div(info[which], 3), 2)


def cut_out(info, trailing, tiles_sent, tiles, columns_sent, columns, sems):
    copies = []

    def copy(a, b):
        copies.append(pltpu.make_async_copy(a, b, sems.at[len(copies)]))
        copies[-1].start()

    for k, (i, j, _) in enumerate(TILE_PARTS):
        rows = pl.ds(tile_start(info, i), B)
        for out, half in ((tiles_sent, 1 - info[4]), (tiles, info[4])):
            copy(trailing.at[rows, half_lanes(tile_start(info, j), half)], out.at[:, lanes_at(k)])
    for j in (0, 1):
        for out, half in ((columns_sent, 1 - info[4]), (columns, info[4])):
            copy(trailing.at[:, half_lanes(tile_start(info, j), half)], out.at[:, lanes_at(j)])
    for c in copies:
        c.wait()


def rows_to_sum(info, trailing, earlier, earlier_other, share, sems):
    n = trailing.shape[1]
    jobs = []
    for j in (0, 1):
        pairs = [(trailing.at[pl.ds(tile_start(info, j), B), :], share.at[:, pl.ds(j * n, n)])]
        jobs.append((lax.div(info[j], 3) == info[2], pairs, j * n))
    pairs = []
    for t in range(3):
        rows = pl.ds(t * B, B)
        pairs.append((earlier.at[rows, :], share.at[:, pl.ds(2 * n + t * B, HALF)]))
        pairs.append((earlier_other.at[rows, :], share.at[:, pl.ds(2 * n + t * B + HALF, HALF)]))
    jobs.append((info[3] == info[2], pairs, 2 * n))
    at = 0
    for held, pairs, start in jobs:
        sem = [sems.at[at + i] for i in range(len(pairs))]
        at += len(pairs)

        @pl.when(held)
        def _():
            parts = [pltpu.make_async_copy(a, b, s) for (a, b), s in zip(pairs, sem)]
            for c in parts:
                c.start()
            for c in parts:
                c.wait()

        @pl.when(jnp.logical_not(held))
        def _():
            share[:, start : start + n] = jnp.zeros((B, n), BF16)


def keep_tiles(info, tiles, earlier, got, out, sems):
    copies = [
        pltpu.make_async_copy(earlier.at[pl.ds(tile_start(info, i), B), :], out.at[:, lanes_at(2 * i + 1)], sems.at[i])
        for i in (0, 1)
    ]
    for c in copies:
        c.start()
    for k, (_, j, place) in enumerate(TILE_PARTS):
        mine = pltpu.make_async_copy(tiles.at[:, lanes_at(k)], out.at[:, lanes_at(place)], sems.at[2 + k])
        theirs = pltpu.make_async_copy(got.at[:, lanes_at(k)], out.at[:, lanes_at(place)], sems.at[2 + k])
        here = owner_core(info, j) == info[4]
        pl.when(here)(mine.start)
        pl.when(jnp.logical_not(here))(theirs.start)
        copies.append(mine)
    for c in copies:
        c.wait()


def keep_columns(info, columns, got, out, sems):
    copies = []
    for j in (0, 1):
        mine = pltpu.make_async_copy(columns.at[:, lanes_at(j)], out.at[:, lanes_at(j)], sems.at[j])
        theirs = pltpu.make_async_copy(got.at[:, lanes_at(j)], out.at[:, lanes_at(j)], sems.at[j])
        here = owner_core(info, j) == info[4]
        pl.when(here)(mine.start)
        pl.when(jnp.logical_not(here))(theirs.start)
        copies.append(mine)
    for c in copies:
        c.wait()


def copy_call(kernel, shapes, info, args, count, out_spaces):
    return pl.pallas_call(
        kernel,
        out_shape=[jax.ShapeDtypeStruct(shape, BF16) for shape in shapes],
        in_specs=[pl.BlockSpec(memory_space=pltpu.SMEM)] + [pl.BlockSpec(memory_space=pl.ANY)] * len(args),
        out_specs=[pl.BlockSpec(memory_space=space) for space in out_spaces],
        scratch_shapes=[pltpu.SemaphoreType.DMA((count,))],
        compiler_params=pltpu.CompilerParams(vmem_limit_bytes=16 << 20),
        cost_estimate=pl.CostEstimate(flops=10**6, bytes_accessed=1 << 20, transcendentals=0),
        name=kernel.__name__,
    )(info, *args)


barrier = lax.optimization_barrier


def swap(x, axis, mask):
    size = lax.axis_size(axis)
    return lax.ppermute(x, axis, [(i, i ^ mask) for i in range(size)])


def lane_roots(width, parts):
    lane = lax.broadcasted_iota(jnp.int32, (1, width), 1)
    out = jnp.full((1, width), parts[-1][1], jnp.int32)
    for end, root in reversed(parts[:-1]):
        out = jnp.where(lane < end, root, out)
    return out


def ring_sends(chunks, me):
    return tuple(lax.dynamic_index_in_dim(chunks, me ^ k, 0, keepdims=False) for k in (1, 2, 3))


def ring_moves(sent, axis, step):
    return tuple(swap(x, axis, k * step) for x, k in zip(sent, (1, 2, 3)))


def ring_pick(chunks, got, me, root):
    out = lax.dynamic_index_in_dim(chunks, me, 0, keepdims=False)
    for k in (1, 2, 3):
        out = jnp.where((me ^ root) == k, got[k - 1], out)
    return out


def ring_take(chunks, axis, step, me, root):
    return ring_pick(chunks, barrier(ring_moves(barrier(ring_sends(chunks, me)), axis, step)), me, root)


def ring_parts(x, got, me):
    parts = []
    for k in range(4):
        other = me ^ k
        parts.append(
            jnp.where(other == 0, x, jnp.where(other == 1, got[0], jnp.where(other == 2, got[1], got[2])))
        )
    return jnp.concatenate(parts, 0)


def ring_join(x, axis, step, me):
    return ring_parts(x, barrier(ring_moves((x, x, x), axis, step)), me)


def gray(x, bit):
    return ((x >> bit) ^ (x >> (bit + 1))) & 1


def halves(x, bit):
    n = x.shape[0] // 2
    return lax.dynamic_slice_in_dim(x, (1 - bit) * n, n, 0), lax.dynamic_slice_in_dim(x, bit * n, n, 0)


def as_one_step(here, f, *args):
    def nothing(*xs):
        return jax.tree.map(lambda o: jnp.zeros(o.shape, o.dtype), jax.eval_shape(f, *xs))

    return lax.cond(here, f, nothing, *args)


def body(trailing, earlier, block_order):
    z = lax.axis_index("col")
    d = lax.axis_index("depth")
    r = lax.axis_index("row")
    g = 2 * z + d
    n = trailing.shape[0]
    count = n // B
    p0, p1 = block_order[0], block_order[1]
    g0, g1 = p0 // count, p1 // count
    z0, z1 = g0 >> 1, g1 >> 1
    x_here, y_here = r >> 2, r & 3
    info = jnp.stack([p0, p1, r, g, d]).astype(jnp.int32)

    earlier_other = swap(earlier, "depth", 1)
    shapes = [(B, 3 * HALF)] * 2 + [(n, B)] * 2
    tiles_sent, tiles, columns_sent, columns = copy_call(cut_out, shapes, info, (trailing,), 10, [pl.ANY] * 4)
    got, columns_sent = barrier((swap(tiles_sent, "depth", 1), columns_sent))
    columns_got = swap(columns_sent, "depth", 1)
    (pay,) = copy_call(keep_tiles, [(B, 5 * HALF)], info, (tiles, earlier, got), 5, [pl.ANY])
    width = pay.shape[1]
    row_root = lane_roots(width, [(2 * HALF, g0), (width, g1)])
    col_root = lane_roots(width, [(HALF, z0), (2 * HALF, z), (3 * HALF, z0), (4 * HALF, z), (width, z1)])
    chunks = pay.reshape(4, B // 4, width)
    sent, info_b = barrier((ring_sends(chunks, y_here), info))
    moved = ring_moves(sent, "row", 1)

    (column,) = copy_call(keep_columns, [(n, B)], info_b, (columns, columns_got), 2, [pl.ANY])
    column_root = lane_roots(B, [(HALF, z0), (B, z1)])
    b1, b2, b3 = gray(z, 0), gray(z, 1), z >> 2
    away, kept = halves(column, b1)

    (share,) = copy_call(
        rows_to_sum, [(B, 3 * n)], info_b, (trailing, earlier, earlier_other), 8, [pltpu.VMEM]
    )
    moved, away, kept, share = barrier((moved, away, kept, share))
    across = lax.psum(share, "row")
    here = p0 >= 0

    def scatter(moved):
        out = ring_pick(chunks, moved, y_here, row_root & 3)
        out = ring_take(out.reshape(4, B // 16, width), "row", 4, x_here, row_root >> 2)
        got = barrier(ring_moves((out,) * 3, "col", 1))
        for k in (1, 2, 3):
            out = jnp.where(((z ^ col_root) & 3) == k, got[k - 1], out)
        return out

    def gather(out):
        out = jnp.where(b3 != col_root >> 2, swap(out, "col", 7), out)
        out = ring_join(out, "row", 4, x_here)
        out = ring_join(out, "row", 1, y_here)
        return out, swap(out, "depth", 1)

    def factors(moved, away, kept):
        got = swap(away, "col", 1)
        state = as_one_step(here, scatter, moved)
        state, got = barrier((state, got))
        away, kept = halves(jnp.where(gray(column_root, 0) != b1, got, kept), b2)
        state, away = barrier((state, away))
        got = swap(away, "col", 3)
        pay, other = as_one_step(here, gather, state)
        pay, other, got = barrier((pay, other, got))
        part = jnp.where(gray(column_root, 1) != b2, got, kept)
        pay, part = barrier((pay, part))
        got = swap(part, "col", 7)
        state = tuple(tile_call(first_factor, [NARROW] * 4 + [WIDE], 2, (pay, other), info))
        state, got = barrier((state, got))
        f0, i0h, i0l, lp1, work = state
        part = jnp.where(b3 != column_root >> 2, got, part)
        work, part = barrier((work, part))
        got = ring_moves((part,) * 3, "col", 1)
        state = tuple(tile_call(second_factor, [NARROW] * 3, 2, (work,)))
        state, got = barrier((state, got))
        f1, i1h, i1l = state
        whole = ring_parts(part, (got[2], got[0], got[1]), 2 * b1 + b2)
        return whole, pay, other, f0, i0h, i0l, lp1, f1, i1h, i1l

    column, pay, other, f0, i0h, i0l, lp1, f1, i1h, i1l = as_one_step(here, factors, moved, away, kept)
    column_other = swap(column, "depth", 1)
    l0t, l1t = columns_of(across, pay, other, i0h, i0l, lp1, i1h, i1l)
    panels, out = update(
        info,
        [trailing, column, column_other, earlier, earlier_other],
        across,
        [l0t, l1t],
        pay,
        other,
        [f0, i0h, i0l, lp1, f1, i1h, i1l],
    )
    return panels, out


def solution(mesh):
    placed = (P("row", ("col", "depth")), P("row", "depth"), P())
    return jax.shard_map(
        body,
        mesh=mesh,
        in_specs=placed,
        out_specs=(P("row", "depth"), P("row", ("col", "depth"))),
        check_vma=False,
    )
```
